256 devices in a mesh: dp: 64 (over x, z, core), sub: 4 (over y).
Axes of the slice: x: 4, y: 4, z: 8, core: 2. Of those that a mesh axis runs over, the one named last changes fastest.
Arguments:
- tokens: bfloat16 [32768, 512], P('dp', 'sub'), may hold values from -6 to 6
- lengths: int32 [128], replicated, may hold values from 1 to 512, 32768 in all
- weight_in: bfloat16 [512, 2048], P(None, 'sub'), may hold values from -0.25 to 0.25
- weight_out: bfloat16 [512, 512], P('sub'), may hold values from -0.25 to 0.25
- grad_out: bfloat16 [32768, 512], P('dp', 'sub'), may hold values from -6 to 6
Outputs:
- layer_output: bfloat16 [32768, 512], P('dp', 'sub')
- grad_tokens: bfloat16 [32768, 512], P('dp', 'sub')
- grad_win: float32 [512, 2048], P(None, 'sub')
- grad_wout: float32 [512, 512], P('sub')
The draws below stay inside these ranges and needn't reach their ends.
Inputs may be any that keep to these rules, and one draw needn't show every extreme that they name: The 128 lengths sum to 32768; histories lie end to end in order, so one may begin on one index of dp and end on the next; the longest is exactly 512.
All inputs are finite; a program needn't handle non-finite values.
Results may differ from the reference program's by a relative error of at most 0.0076.
Values may be sent and summed in bfloat16 or wider, within the bound.
A program may use at most 64 MiB of HBM per device.

```python
import math
import jax
import jax.numpy as jnp
import numpy as np
from jax import lax

D = 512
HEADS = 4
HEAD_DIM = 128
MAXLEN = 512
TOKENS = 32768
SEQS = 128


def shard_levels(key, extent, cuts, least, top_value):
    loudness = 1.0
    for dim, parts in cuts:
        draws = jax.random.uniform(jax.random.fold_in(jax.random.fold_in(key, 6), dim), (parts,), jnp.float32, least / len(cuts), top_value / len(cuts))
        loudness = loudness * jnp.repeat(jnp.exp(draws), extent[dim] // parts).reshape((-1,) + (1,) * (len(extent) - 1 - dim))
    return loudness


def length_profile(count, total, limit, lean):
    loads = [(1 << 20) // math.isqrt(grade ** lean) + 1 for grade in range(2, count + 1)]
    spare, holding = total - limit - (count - 1), [1] * (count - 1)
    while spare > 0:
        candidates = [i for i in range(count - 1) if holding[i] < limit]
        pool, budget = sum([loads[i] for i in candidates]), spare
        for i in candidates:
            extra = min(limit - holding[i], max(1, budget * loads[i] // pool), spare)
            holding[i] = holding[i] + extra
            spare = spare - extra
    return np.array([limit] + holding)


def uneven(key, amount, total, reach, lean):
    if amount == 2:
        one = jax.random.randint(key, (), max(1, total - reach), min(reach, total - 1) + 1)
        return jnp.stack([one, total - one])
    sizes = jnp.asarray(length_profile(amount, total, reach, lean), jnp.int32)
    twos = (amount - 1) // 2
    donor, sink = sizes[1:1 + 2 * twos:2], sizes[2:2 + 2 * twos:2]
    slack = jnp.minimum(donor - 1, reach - sink)
    shifted = jax.random.randint(jax.random.fold_in(key, 1), (twos,), 0, 1 << 20) % (slack + 1)
    sizes = sizes.at[1:1 + 2 * twos:2].set(donor - shifted).at[2:2 + 2 * twos:2].set(sink + shifted)
    return sizes[jax.random.permutation(jax.random.fold_in(key, 2), amount)]


def bell_draw(key, extent, spread, bound, shards=(), kind=jnp.bfloat16):
    array = spread * jax.random.normal(key, extent, jnp.float32)
    if shards:
        array = array * shard_levels(key, extent, shards, -0.22, 0.18)
    return jnp.clip(array, -bound, bound).astype(kind)


def setup_inputs(seed: int = 0) -> dict:
    splits = jax.random.split(jax.random.key(seed), 6)
    tokens = bell_draw(splits[0], (TOKENS, D), 1.0, 6.0, ((0, 64), (1, 4)))
    lengths = uneven(splits[1], SEQS, TOKENS, MAXLEN, 2).astype(jnp.int32)
    weight_in = bell_draw(splits[2], (D, 4 * D), D ** -0.5, 0.25, ((1, 4),))
    weight_out = bell_draw(splits[3], (D, D), D ** -0.5, 0.25, ((0, 4),))
    grad_out = bell_draw(splits[4], (TOKENS, D), 1.0, 6.0, ((0, 64), (1, 4)))
    return dict(tokens=tokens, lengths=lengths, weight_in=weight_in, weight_out=weight_out, grad_out=grad_out)


EPSILON = 1e-05

def norm_rows(values):
    row_mean = lax.optimization_barrier(jnp.mean(values, axis=1, keepdims=True))
    centred = values - row_mean
    inv_std = lax.rsqrt(lax.optimization_barrier(jnp.mean(centred * centred, axis=1, keepdims=True)) + EPSILON)
    return (centred * inv_std, inv_std)

def silu_slope(values):
    sigmoid = jax.nn.sigmoid(values)
    return sigmoid * (1.0 + values * (1.0 - sigmoid))

def reference(tokens, lengths, weight_in, weight_out, grad_out):
    x_hat, x_scale = norm_rows(tokens.astype(jnp.float32))
    x_normed = x_hat.astype(jnp.bfloat16)
    hidden = jnp.dot(x_normed, weight_in, preferred_element_type=jnp.float32)
    projected = lax.optimization_barrier(jax.nn.silu(hidden).astype(jnp.bfloat16))
    grouped = projected.reshape(TOKENS, HEADS, 4, HEAD_DIM)
    gate_u = grouped[:, :, 0].reshape(TOKENS, D).astype(jnp.float32)
    values = grouped[:, :, 1].astype(jnp.float32)
    queries = grouped[:, :, 2].astype(jnp.float32)
    key_rows = grouped[:, :, 3].astype(jnp.float32)
    seq_ends = jnp.cumsum(lengths).astype(jnp.int32)
    starts = (seq_ends - lengths).astype(jnp.int32)
    position = jnp.arange(MAXLEN, dtype=jnp.int32)
    causal = position[None, :] <= position[:, None]
    padding = jnp.zeros((MAXLEN, HEADS, HEAD_DIM), jnp.float32)

    def extend(source):
        return jnp.concatenate([source, padding], 0)
    q_long = extend(queries)
    k_long = extend(key_rows)
    v_long = extend(values)

    def window(source, start_row):
        return lax.dynamic_slice_in_dim(source, start_row, MAXLEN, 0)

    def tile(start_row, seq_length):
        q_rows = window(q_long, start_row)
        k_rows = window(k_long, start_row)
        v_rows = window(v_long, start_row)
        live_rows = position < seq_length
        allowed = (causal & live_rows[:, None] & live_rows[None, :])[None]
        scores = jnp.einsum('qhd,khd->hqk', q_rows, k_rows) / math.sqrt(HEAD_DIM)
        rounded = lax.optimization_barrier(jnp.where(allowed, jax.nn.silu(scores), 0.0).astype(jnp.bfloat16))
        return (q_rows, k_rows, v_rows, scores, allowed, rounded.astype(jnp.float32))

    def forward_step(summed, seq_item):
        start_row, seq_length = seq_item
        pieces = tile(start_row, seq_length)
        attended = jnp.einsum('hqk,khd->qhd', pieces[5], pieces[2])
        summed = lax.dynamic_update_slice_in_dim(summed, window(summed, start_row) + attended, start_row, 0)
        return (summed, jnp.zeros((), jnp.float32))
    initial = jnp.zeros((TOKENS + MAXLEN, HEADS, HEAD_DIM), jnp.float32)
    attended = lax.scan(forward_step, initial, (starts, lengths))[0]
    attended = attended[:TOKENS].reshape(TOKENS, D)
    normed, av_scale = norm_rows(attended)
    gated = (normed * gate_u).astype(jnp.bfloat16)
    layer_output = (tokens.astype(jnp.float32) + jnp.dot(gated, weight_out, preferred_element_type=jnp.float32)).astype(jnp.bfloat16)
    d_gated = jnp.dot(grad_out, weight_out.T, preferred_element_type=jnp.float32)
    grad_wout = jnp.dot(gated.T, grad_out, preferred_element_type=jnp.float32) / math.sqrt(TOKENS)
    d_normed = d_gated * gate_u
    d_gate = d_gated * normed
    d_attended = av_scale * (d_normed - lax.optimization_barrier(jnp.mean(d_normed, axis=1, keepdims=True)) - normed * lax.optimization_barrier(jnp.mean(d_normed * normed, axis=1, keepdims=True)))
    d_rounded = lax.optimization_barrier(d_attended.astype(jnp.bfloat16))
    g_long = extend(d_rounded.reshape(TOKENS, HEADS, HEAD_DIM).astype(jnp.float32))

    def backward_step(carried, seq_item):
        grad_q, grad_k, grad_v = carried
        start_row, seq_length = seq_item
        q_rows, k_rows, v_rows, scores, allowed, weights = tile(start_row, seq_length)
        g_rows = window(g_long, start_row)
        d_weight = jnp.einsum('qhd,khd->hqk', g_rows, v_rows)
        d_score = jnp.where(allowed, d_weight * silu_slope(scores), 0.0) / math.sqrt(HEAD_DIM)
        d_score = lax.optimization_barrier(d_score.astype(jnp.bfloat16)).astype(jnp.float32)
        new_q = jnp.einsum('hqk,khd->qhd', d_score, k_rows)
        new_k = jnp.einsum('hqk,qhd->khd', d_score, q_rows)
        new_v = jnp.einsum('hqk,qhd->khd', weights, g_rows)
        grad_q = lax.dynamic_update_slice_in_dim(grad_q, window(grad_q, start_row) + new_q, start_row, 0)
        grad_k = lax.dynamic_update_slice_in_dim(grad_k, window(grad_k, start_row) + new_k, start_row, 0)
        grad_v = lax.dynamic_update_slice_in_dim(grad_v, window(grad_v, start_row) + new_v, start_row, 0)
        return ((grad_q, grad_k, grad_v), jnp.zeros((), jnp.float32))
    grads = lax.scan(backward_step, (initial, initial, initial), (starts, lengths))[0]
    grad_q = grads[0][:TOKENS]
    grad_k = grads[1][:TOKENS]
    grad_v = grads[2][:TOKENS]
    stacked = jnp.stack([d_gate.reshape(TOKENS, HEADS, HEAD_DIM), grad_v, grad_q, grad_k], 2)
    d_hidden = (stacked.reshape(TOKENS, 4 * D) * silu_slope(hidden)).astype(jnp.bfloat16)
    grad_win = jnp.dot(x_normed.T, d_hidden, preferred_element_type=jnp.float32) / math.sqrt(TOKENS)
    d_input = jnp.dot(d_hidden, weight_in.T, preferred_element_type=jnp.float32)
    d_tokens = grad_out.astype(jnp.float32) + x_scale * (d_input - lax.optimization_barrier(jnp.mean(d_input, axis=1, keepdims=True)) - x_hat * lax.optimization_barrier(jnp.mean(d_input * x_hat, axis=1, keepdims=True)))
    return (layer_output, d_tokens.astype(jnp.bfloat16), grad_win, grad_wout)
```

```python
import functools
import math

import jax
import jax.numpy as jnp
from jax import lax
from jax.experimental import pallas as pl
from jax.experimental.pallas import tpu as pltpu
from jax.sharding import PartitionSpec as P

EPSILON = 1e-05
NX, NZ, NC, NY = 4, 8, 2, 4
ROWS, HEAD, WIDTH = 512, 128, 512
TILE = 128
MESH = pl.DeviceIdType.MESH
BF, F32 = jnp.bfloat16, jnp.float32

NN = (((1,), (0,)), ((), ()))
NT = (((1,), (1,)), ((), ()))
TN = (((0,), (0,)), ((), ()))


def mm(left, right, dims=NN):
    return lax.dot_general(left, right, dims, preferred_element_type=F32)


class Sender:
    def __init__(self, send_sem, recv_sem):
        self.send_sem, self.recv_sem, self.copies = send_sem, recv_sem, []

    def __call__(self, src, dst, device):
        i = len(self.copies)
        copy = pltpu.make_async_remote_copy(
            src_ref=src,
            dst_ref=dst,
            send_sem=self.send_sem.at[i],
            recv_sem=self.recv_sem.at[i],
            device_id=device,
            device_id_type=MESH,
        )
        copy.start()
        self.copies.append(copy)
        return copy


class Reduce:
    def __init__(self, send, place, refs, scale):
        self.send, self.scale = send, scale
        self.x, self.z, self.c, self.at = place
        self.part, self.sb, self.rc, self.sx, self.rx, self.sz, self.rz, self.full = refs
        self.dt = self.full.dtype

    def s1(self):
        c = self.c
        self.sb[...] = self.part[1 - c].astype(self.dt)
        self.w1 = self.send(self.sb, self.rc, self.at(self.x, self.z, 1 - c))

    def s2(self):
        self.w1.wait_recv()
        total = self.part[self.c] + self.rc[...].astype(F32)
        self.part[self.c] = total
        self.sx[...] = total.astype(self.dt)
        self.w2 = []
        for r in (1, 3, 2):
            to = lax.rem(self.x + r, NX)
            self.w2.append(
                self.send(self.sx.at[to], self.rx.at[r - 1], self.at(to, self.z, self.c))
            )

    def s3(self):
        for w in self.w2:
            w.wait_recv()
        total = self.part[self.c, self.x]
        for r in range(NX - 1):
            total = total + self.rx[r].astype(F32)
        self.part[self.c, self.x] = total
        self.sz[...] = total.astype(self.dt)
        self.w3 = []
        for r in (1, 7, 2, 6, 3, 5, 4):
            to = lax.rem(self.z + r, NZ)
            self.w3.append(
                self.send(self.sz.at[to], self.rz.at[r - 1], self.at(self.x, to, self.c))
            )

    def s4(self):
        for w in self.w3:
            w.wait_recv()
        total = self.part[self.c, self.x, self.z]
        for r in range(NZ - 1):
            total = total + self.rz[r].astype(F32)
        mine = (self.c, self.x, self.z)
        self.full[mine] = (total * self.scale).astype(self.dt)
        self.w4 = []
        for r in (1, 7, 2, 6, 3, 5, 4):
            to = lax.rem(self.z + r, NZ)
            self.w4.append(
                self.send(self.full.at[mine], self.full.at[mine], self.at(self.x, to, self.c))
            )

    def s5(self):
        for w in self.w4:
            w.wait_recv()
        mine = (self.c, self.x)
        self.w5 = []
        for r in (1, 3, 2):
            to = lax.rem(self.x + r, NX)
            self.w5.append(
                self.send(self.full.at[mine], self.full.at[mine], self.at(to, self.z, self.c))
            )

    def s6(self):
        for w in self.w5:
            w.wait_recv()
        self.w6 = self.send(
            self.full.at[self.c], self.full.at[self.c], self.at(self.x, self.z, 1 - self.c)
        )

    def s7(self):
        self.w6.wait_recv()


def column(value):
    return jnp.sum(value, axis=1, keepdims=True)


def start_rows(lens_ref, first_row):
    lens = jnp.broadcast_to(lens_ref[...].astype(F32), (128, 128))
    down = lax.broadcasted_iota(jnp.int32, (128, 128), 0)
    across = lax.broadcasted_iota(jnp.int32, (128, 128), 1)
    as_column = column(jnp.where(down == across, lens, 0.0))
    starts = jnp.sum(jnp.where(down < across, as_column, 0.0), axis=0, keepdims=True)
    rows = (first_row + lax.broadcasted_iota(jnp.int32, (ROWS, 128), 0)).astype(F32)
    own = jnp.max(jnp.where(starts <= rows, starts, 0.0), axis=1, keepdims=True)
    return own - first_row.astype(F32)


def kernel(
    tok, lens, win, wout, gout,
    lo, gt, gwin, gwout,
    xg, gg, wc, xh, xo, xn, xnt, xr, proj, slope, kv, srow,
    w_own, w_prev, sl_own, sl_prev, ds_own, ds_prev,
    stat, gat, datt, dgate, dq, dk, dv, dkv_s, dkv_r,
    din, din_s, din_r, stat2, dhid,
    *rest,
):
    reduce_refs, (send_sem, recv_sem) = rest[:-2], rest[-2:]
    d, y = lax.axis_index("dp"), lax.axis_index("sub")
    c = lax.rem(d, NC)
    z = lax.rem(d // NC, NZ)
    x = d // (NC * NZ)
    ndp = NX * NZ * NC

    def at(ax, az, ac):
        return ((ax * NZ + az) * NC + ac, y)

    above = (lax.rem(d + 1, ndp), y)
    below = (lax.rem(d + ndp - 1, ndp), y)
    y_peers = [(r, lax.rem(y + r, NY)) for r in (1, 3, 2)]

    barrier = pltpu.get_barrier_semaphore()
    greet = [(d, peer) for _, peer in y_peers]
    greet += [at(lax.rem(x + r, NX), z, c) for r in range(1, NX)]
    greet += [at(x, lax.rem(z + r, NZ), c) for r in range(1, NZ)]
    greet += [at(x, z, 1 - c)]
    greet += [(lax.rem(d + ndp + 2 * c - 1, ndp), y)]
    for device in greet:
        pl.semaphore_signal(barrier, inc=1, device_id=device, device_id_type=MESH)
    pl.semaphore_wait(barrier, len(greet))

    send = Sender(send_sem, recv_sem)
    place = (x, z, c, at)
    scaling = 1.0 / math.sqrt(ROWS * ndp)
    sums = [Reduce(send, place, reduce_refs[8 * i : 8 * i + 8], scaling) for i in range(3)]
    r_out, r_uq, r_vk = sums

    got_x = [send(tok, xg.at[y], (d, peer)) for _, peer in y_peers]
    got_g = [send(gout, gg.at[y], (d, peer)) for _, peer in y_peers]
    got_w = [
        send(
            wout.at[:, pl.ds(pl.multiple_of(peer * HEAD, HEAD), HEAD)],
            wc.at[y],
            (d, peer),
        )
        for _, peer in y_peers
    ]
    xg[y] = tok[...]
    gg[y] = gout[...]
    wc[y] = wout[:, pl.ds(pl.multiple_of(y * HEAD, HEAD), HEAD)]
    srow[...] = jnp.broadcast_to(start_rows(lens, d * ROWS), (ROWS, 128))
    for w in got_x:
        w.wait_recv()

    @pl.loop(0, ROWS // TILE)
    def _(t):
        rows = pl.ds(pl.multiple_of(t * TILE, TILE), TILE)
        parts = [xg[b, rows, :].astype(F32) for b in range(NY)]
        mean = column(parts[0] + parts[1] + parts[2] + parts[3]) * (1.0 / WIDTH)
        parts = [part - mean for part in parts]
        var = column(sum(part * part for part in parts)) * (1.0 / WIDTH)
        inv = lax.rsqrt(var + EPSILON)
        xr[rows, :] = jnp.broadcast_to(inv, (TILE, 128))
        for b in range(NY):
            hat = parts[b] * inv
            xh[b, rows, :] = hat
            xn[rows, b * HEAD : (b + 1) * HEAD] = hat.astype(BF)

    def project(g):
        hidden = mm(xn[...], win[:, g * HEAD : (g + 1) * HEAD])
        sig = 0.5 * jnp.tanh(0.5 * hidden) + 0.5
        proj[g] = (hidden * sig).astype(BF)
        slope[g] = sig * (1.0 + hidden * (1.0 - sig))

    project(3)
    got_k = send(proj.at[3], kv.at[1], above)
    project(1)
    got_v = send(proj.at[1], kv.at[0], above)
    project(2)

    root = 1.0 / math.sqrt(HEAD)

    def attend(q_rows, k_rows, t, width, shift, causal):
        scores = mm(q_rows, k_rows, NT) * root
        col = lax.broadcasted_iota(jnp.int32, (TILE, width), 1)
        begin = srow[t * TILE : (t + 1) * TILE, 0:1].astype(jnp.int32) + shift
        allowed = col >= begin
        if causal:
            row = lax.broadcasted_iota(jnp.int32, (TILE, width), 0) + t * TILE
            allowed = allowed & (col <= row)
        sig = 0.5 * jnp.tanh(0.5 * scores) + 0.5
        weight = jnp.where(allowed, scores * sig, 0.0).astype(BF)
        tangent = jnp.where(allowed, sig * (1.0 + scores * (1.0 - sig)) * root, 0.0)
        return weight, tangent

    for t in range(ROWS // TILE):
        rows, n = slice(t * TILE, (t + 1) * TILE), (t + 1) * TILE
        weight, tangent = attend(proj[2, rows], proj[3, :n], t, n, 0, True)
        w_own[rows, :n] = weight
        sl_own[rows, :n] = tangent
        din[0, rows] = mm(weight, proj[1, :n])

    project(0)
    for w in got_g:
        w.wait_recv()
    gate = proj[0].astype(F32)
    d_gated = sum(
        mm(gg[b], wout[:, b * HEAD : (b + 1) * HEAD], NT) for b in range(NY)
    )
    dgate[...] = d_gated
    e = d_gated * gate
    din[1] = e

    got_k.wait_recv()
    got_v.wait_recv()
    for t in range(ROWS // TILE):
        rows = slice(t * TILE, (t + 1) * TILE)
        weight, tangent = attend(proj[2, rows], kv[1], t, ROWS, ROWS, False)
        w_prev[rows, :] = weight
        sl_prev[rows, :] = tangent
        din[0, rows] = din[0, rows] + mm(weight, kv[0])

    a = din[0]
    e = din[1]
    sum_a = column(a)
    ca = a - sum_a * (1.0 / HEAD)
    lane = lax.broadcasted_iota(jnp.int32, (ROWS, 128), 1)
    packed = jnp.where(
        lane == 0, sum_a,
        jnp.where(lane == 1, column(ca * ca),
                  jnp.where(lane == 2, column(e), jnp.where(lane == 3, column(e * ca), 0.0))),
    )
    stat[y] = packed.T[:8]
    got_s = [send(stat.at[y], stat.at[y], (d, peer)) for _, peer in y_peers]
    xnt[...] = xn[...].T
    for w in got_s:
        w.wait_recv()
    heads = [stat[h] for h in range(NY)]
    mean = sum(h[0:1] for h in heads) * (1.0 / WIDTH)
    var, s_e, s_en = 0.0, 0.0, 0.0
    for h in heads:
        off = h[0:1] * (1.0 / HEAD) - mean
        var = var + h[1:2] + HEAD * off * off
        s_e = s_e + h[2:3]
        s_en = s_en + h[3:4] + off * h[2:3]
    inv = lax.rsqrt(var * (1.0 / WIDTH) + EPSILON)
    line = lax.broadcasted_iota(jnp.int32, (128, ROWS), 0)
    back = jnp.where(
        line == 0, mean,
        jnp.where(line == 1, inv,
                  jnp.where(line == 2, s_e * (1.0 / WIDTH),
                            jnp.where(line == 3, s_en * inv * (1.0 / WIDTH), 0.0))),
    ).T
    mean, inv, s_e, s_en = [back[:, i : i + 1] for i in range(4)]
    normed = (din[0] - mean) * inv
    datt[...] = (inv * (din[1] - s_e - normed * s_en)).astype(BF)
    gat[y] = (normed * proj[0].astype(F32)).astype(BF)
    got_a = [send(gat.at[y], gat.at[y], (d, peer)) for _, peer in y_peers]
    dhid[:, 0:HEAD] = (dgate[...] * normed * slope[0]).astype(BF)

    for t in range(ROWS // TILE):
        rows = slice(t * TILE, (t + 1) * TILE)
        ds = (mm(datt[rows], kv[0], NT) * sl_prev[rows, :]).astype(BF)
        ds_prev[rows, :] = ds
        dq[rows, :] = mm(ds, kv[1])
    dkv_s[0] = mm(w_prev[...], datt[...], TN).astype(BF)
    got_dv = send(dkv_s.at[0], dkv_r.at[0], below)
    dkv_s[1] = mm(ds_prev[...], proj[2], TN).astype(BF)
    got_dk = send(dkv_s.at[1], dkv_r.at[1], below)

    gated = gat[y]
    gated_t = gated.T
    for b in range(NY):
        r_out.part[b // 2, (b % 2) * 2 : (b % 2) * 2 + 2] = mm(gated_t, gg[b]).reshape(2, NZ, 8, HEAD)
    r_out.s1()

    for t in range(ROWS // TILE):
        rows, n = slice(t * TILE, (t + 1) * TILE), (t + 1) * TILE
        ds = (mm(datt[rows], proj[1, :n], NT) * sl_own[rows, :n]).astype(BF)
        ds_own[rows, :n] = ds
        dq[rows, :] = dq[rows, :] + mm(ds, proj[3, :n])
    dhid[:, 2 * HEAD : 3 * HEAD] = (dq[...] * slope[2]).astype(BF)
    for i, g in enumerate((0, 2)):
        r_uq.part[i] = mm(xnt[...], dhid[:, g * HEAD : (g + 1) * HEAD]).reshape(NX, NZ, 16, HEAD)
    r_uq.s1()
    r_out.s2()
    for t in range(ROWS // TILE):
        cols = slice(t * TILE, (t + 1) * TILE)
        dk[cols, :] = mm(ds_own[t * TILE :, cols], proj[2, t * TILE :], TN)
        dv[cols, :] = mm(w_own[t * TILE :, cols], datt[t * TILE :], TN)
    r_uq.s2()
    got_dv.wait_recv()
    dhid[:, HEAD : 2 * HEAD] = ((dv[...] + dkv_r[0].astype(F32)) * slope[1]).astype(BF)
    got_dk.wait_recv()
    dhid[:, 3 * HEAD :] = ((dk[...] + dkv_r[1].astype(F32)) * slope[3]).astype(BF)
    for i, g in enumerate((1, 3)):
        r_vk.part[i] = mm(xnt[...], dhid[:, g * HEAD : (g + 1) * HEAD]).reshape(NX, NZ, 16, HEAD)
    r_vk.s1()

    one, two = 0.0, 0.0
    for b in range(NY):
        part = mm(dhid[...], win[b * HEAD : (b + 1) * HEAD, :], NT)
        one = one + part
        two = two + part * xh[b]
        din[b] = part
        din_s[b] = part.astype(BF)
    packed = jnp.where(lane == 0, column(one), jnp.where(lane == 1, column(two), 0.0))
    stat2[y] = packed.T[:8]
    got_i = [send(din_s.at[peer], din_r.at[r - 1], (d, peer)) for r, peer in y_peers]
    got_t = [send(stat2.at[y], stat2.at[y], (d, peer)) for _, peer in y_peers]
    r_uq.s3()
    r_vk.s2()
    r_out.s3()

    for w in got_a + got_w:
        w.wait_recv()
    lo[...] = (
        tok[...].astype(F32) + sum(mm(gat[h], wc[h]) for h in range(NY))
    ).astype(BF)

    r_uq.s4()
    r_vk.s3()
    r_out.s4()
    r_uq.s5()
    r_vk.s4()
    r_out.s5()

    for w in got_i + got_t:
        w.wait_recv()
    total = din[y]
    for r in range(NY - 1):
        total = total + din_r[r].astype(F32)
    both = (stat2[0] + stat2[1] + stat2[2] + stat2[3]) * (1.0 / WIDTH)
    back = jnp.where(line == 0, both[0:1], jnp.where(line == 1, both[1:2], 0.0)).T
    piece = xr[:, 0:1] * (total - back[:, 0:1] - xh[y] * back[:, 1:2])
    gt[...] = (gout[...].astype(F32) + piece).astype(BF)

    r_uq.s6()
    r_vk.s5()
    r_out.s6()
    r_uq.s7()
    r_vk.s6()
    for i, g in enumerate((0, 2)):
        gwin[:, g * HEAD : (g + 1) * HEAD] = r_uq.full[i].reshape(ROWS, HEAD).astype(F32)
    r_out.s7()
    for b in range(NY):
        block = r_out.full[b // 2, (b % 2) * 2 : (b % 2) * 2 + 2]
        gwout[:, b * HEAD : (b + 1) * HEAD] = block.reshape(HEAD, HEAD)
    r_vk.s7()
    for i, g in enumerate((1, 3)):
        gwin[:, g * HEAD : (g + 1) * HEAD] = r_vk.full[i].reshape(ROWS, HEAD).astype(F32)
    for w in send.copies:
        w.wait_send()


def reduce_scratch(rows, dt):
    return [
        pltpu.VMEM((NC, NX, NZ, rows, HEAD), F32),
        pltpu.VMEM((NX, NZ, rows, HEAD), dt),
        pltpu.VMEM((NX, NZ, rows, HEAD), dt),
        pltpu.VMEM((NX, NZ, rows, HEAD), dt),
        pltpu.VMEM((NX - 1, NZ, rows, HEAD), dt),
        pltpu.VMEM((NZ, rows, HEAD), dt),
        pltpu.VMEM((NZ - 1, rows, HEAD), dt),
        pltpu.VMEM((NC, NX, NZ, rows, HEAD), dt),
    ]


def shards(tokens, lengths, weight_in, weight_out, grad_out):
    lengths = lengths.reshape(1, -1)
    vm = pl.BlockSpec(memory_space=pltpu.VMEM)
    blocks = lambda n, dt: pltpu.VMEM((n, ROWS, HEAD), dt)
    full = lambda dt: pltpu.VMEM((ROWS, WIDTH), dt)
    one = lambda dt: pltpu.VMEM((ROWS, HEAD), dt)
    scratch = [
        blocks(NY, BF), blocks(NY, BF), pltpu.VMEM((NY, HEAD, HEAD), BF),
        blocks(NY, F32), one(F32), full(BF), full(BF), one(F32),
        blocks(4, BF), blocks(4, F32), blocks(2, BF), one(F32),
        full(BF), full(BF), full(F32), full(F32), full(BF), full(BF),
        pltpu.VMEM((NY, 8, ROWS), F32), blocks(NY, BF), one(BF), one(F32),
        one(F32), one(F32), one(F32), blocks(2, BF), blocks(2, BF),
        blocks(NY, F32), blocks(NY, BF), blocks(NY - 1, BF),
        pltpu.VMEM((NY, 8, ROWS), F32), full(BF),
        *reduce_scratch(8, F32), *reduce_scratch(16, BF), *reduce_scratch(16, BF),
        pltpu.SemaphoreType.DMA((100,)), pltpu.SemaphoreType.DMA((100,)),
    ]
    return pl.pallas_call(
        kernel,
        out_shape=(
            jax.ShapeDtypeStruct((ROWS, HEAD), BF),
            jax.ShapeDtypeStruct((ROWS, HEAD), BF),
            jax.ShapeDtypeStruct((WIDTH, 4 * HEAD), F32),
            jax.ShapeDtypeStruct((HEAD, WIDTH), F32),
        ),
        in_specs=[vm] * 5,
        out_specs=(vm,) * 4,
        scratch_shapes=scratch,
        compiler_params=pltpu.CompilerParams(
            collective_id=0, has_side_effects=True, vmem_limit_bytes=48 * 1024 * 1024
        ),
        name="layer",
    )(tokens, lengths, weight_in, weight_out, grad_out)


def solution(mesh):
    placed = (P("dp", "sub"), P(), P(None, "sub"), P("sub", None), P("dp", "sub"))
    return jax.shard_map(
        shards,
        mesh=mesh,
        in_specs=placed,
        out_specs=(P("dp", "sub"), P("dp", "sub"), P(None, "sub"), P("sub", None)),
        check_vma=False,
    )
```

```python
import functools
import math

import jax
import jax.numpy as jnp
from jax import lax
from jax.experimental import pallas as pl
from jax.experimental.pallas import tpu as pltpu
from jax.sharding import PartitionSpec as P

EPSILON = 1e-05
NX, NZ, NC, NY = 4, 8, 2, 4
ROWS, HEAD, WIDTH = 512, 128, 512
TILE = 128
MESH = pl.DeviceIdType.MESH
BF, F32 = jnp.bfloat16, jnp.float32

NN = (((1,), (0,)), ((), ()))
NT = (((1,), (1,)), ((), ()))
TN = (((0,), (0,)), ((), ()))


def mm(left, right, dims=NN):
    return lax.dot_general(left, right, dims, preferred_element_type=F32)


class Sender:
    def __init__(self, send_sem, recv_sem):
        self.send_sem, self.recv_sem, self.copies = send_sem, recv_sem, []

    def __call__(self, src, dst, device):
        i = len(self.copies)
        copy = pltpu.make_async_remote_copy(
            src_ref=src,
            dst_ref=dst,
            send_sem=self.send_sem.at[i],
            recv_sem=self.recv_sem.at[i],
            device_id=device,
            device_id_type=MESH,
        )
        copy.start()
        self.copies.append(copy)
        return copy


class Reduce:
    def __init__(self, send, core, first, second, refs, scale):
        self.send, self.scale = send, scale
        self.c, self.core = core
        self.n1, self.i1, self.at1 = first
        self.n2, self.i2, self.at2 = second
        self.part, self.sb, self.rc, self.s_1, self.r_1, self.s_2, self.r_2, self.full = refs
        self.dt = self.full.dtype

    @staticmethod
    def far_first(n):
        return sorted(range(1, n), key=lambda r: (-min(r, n - r), r))

    def to1(self, r):
        return lax.rem(self.i1 + r, self.n1)

    def to2(self, r):
        return lax.rem(self.i2 + r, self.n2)

    def s1(self, other):
        self.sb[...] = other.astype(self.dt).reshape(self.sb.shape)
        self.w1 = self.send(self.sb, self.rc, self.core)

    def keep(self, own):
        self.part[...] = own.reshape(self.part.shape)

    def s2(self):
        self.w1.wait_recv()
        total = self.part[...] + self.rc[...].astype(F32)
        self.part[...] = total
        self.s_1[...] = total.astype(self.dt)
        self.w2 = []
        for r in self.far_first(self.n1):
            to = self.to1(r)
            self.w2.append(self.send(self.s_1.at[to], self.r_1.at[r - 1], self.at1(to)))

    def s3(self):
        for w in self.w2:
            w.wait_recv()
        total = self.part[self.i1]
        for r in range(self.n1 - 1):
            total = total + self.r_1[r].astype(F32)
        self.part[0] = total
        self.s_2[...] = total.astype(self.dt)
        self.w3 = []
        for r in self.far_first(self.n2):
            to = self.to2(r)
            self.w3.append(self.send(self.s_2.at[to], self.r_2.at[r - 1], self.at2(to)))

    def s4(self):
        for w in self.w3:
            w.wait_recv()
        total = self.part[0, self.i2]
        for r in range(self.n2 - 1):
            total = total + self.r_2[r].astype(F32)
        mine = self.full.at[self.c, self.i1, self.i2]
        self.full[self.c, self.i1, self.i2] = (total * self.scale).astype(self.dt)
        self.w4 = [
            self.send(mine, mine, self.at2(self.to2(r))) for r in self.far_first(self.n2)
        ]

    def s5(self):
        for w in self.w4:
            w.wait_recv()
        mine = self.full.at[self.c, self.i1]
        self.w5 = [
            (r, self.send(mine, mine, self.at1(self.to1(r)))) for r in self.far_first(self.n1)
        ]
        self.w6 = [self.send(mine, mine, self.core)]

    def s6(self):
        for r, w in self.w5[::-1]:
            w.wait_recv()
            piece = self.full.at[self.c, lax.rem(self.i1 + self.n1 - r, self.n1)]
            self.w6.append(self.send(piece, piece, self.core))

    def s7(self):
        for w in self.w6:
            w.wait_recv()


def column(value):
    return jnp.sum(value, axis=1, keepdims=True)


def start_rows(lens_ref, first_row):
    lens = jnp.broadcast_to(lens_ref[...].astype(F32), (128, 128))
    down = lax.broadcasted_iota(jnp.int32, (128, 128), 0)
    across = lax.broadcasted_iota(jnp.int32, (128, 128), 1)
    as_column = column(jnp.where(down == across, lens, 0.0))
    starts = jnp.sum(jnp.where(down < across, as_column, 0.0), axis=0, keepdims=True)
    rows = (first_row + lax.broadcasted_iota(jnp.int32, (ROWS, 128), 0)).astype(F32)
    own = jnp.max(jnp.where(starts <= rows, starts, 0.0), axis=1, keepdims=True)
    return own - first_row.astype(F32)


def kernel(
    tok_h, len_h, win_h, wout_h, gout_h,
    lo, gt, gwin, gwout,
    lens, win, wout,
    xg, gg, wc, xh, xn, xnt, xnp, xr, proj, slope, slope_p, kv, srow,
    w_own, w_prev, sl_own, sl_prev, ds_own, ds_prev,
    stat, gat, att, ee, dgate, datt, dq, dk, dv, dkv_s, dkv_r,
    din, din_s, din_r, stat2, dhid, dh_uq, dh_vk,
    *rest,
):
    reduce_refs, (load_sem, send_sem, recv_sem) = rest[:-3], rest[-3:]
    d, y = lax.axis_index("dp"), lax.axis_index("sub")
    c = lax.rem(d, NC)
    z = lax.rem(d // NC, NZ)
    x = d // (NC * NZ)
    ndp = NX * NZ * NC

    def at(ax, az, ac):
        return ((ax * NZ + az) * NC + ac, y)

    above = (lax.rem(d + 1, ndp), y)
    below = (lax.rem(d + ndp - 1, ndp), y)
    y_peers = [(r, lax.rem(y + r, NY)) for r in (2, 1, 3)]
    y_up, y_down = lax.rem(y + 1, NY), lax.rem(y + NY - 1, NY)

    loads = [
        pltpu.make_async_copy(src, dst, load_sem.at[i])
        for i, (src, dst) in enumerate(
            [
                (tok_h, xg.at[y]), (gout_h, gg.at[y]), (len_h, lens),
                (win_h, win), (wout_h, wout),
            ]
        )
    ]
    for load in loads:
        load.start()

    barrier = pltpu.get_barrier_semaphore()
    greet = [(d, peer) for _, peer in y_peers]
    greet += [at(lax.rem(x + r, NX), z, c) for r in range(1, NX)]
    greet += [at(x, lax.rem(z + r, NZ), c) for r in range(1, NZ)]
    greet += [at(x, z, 1 - c)]
    greet += [(lax.rem(d + ndp + 2 * c - 1, ndp), y)]
    for device in greet:
        pl.semaphore_signal(barrier, inc=1, device_id=device, device_id_type=MESH)
    loads[0].wait()
    loads[1].wait()
    pl.semaphore_wait(barrier, len(greet))

    send = Sender(send_sem, recv_sem)
    core = (c, at(x, z, 1 - c))
    along_x = (NX, x, lambda to: at(to, z, c))
    along_z = (NZ, z, lambda to: at(x, to, c))
    scaling = 1.0 / math.sqrt(ROWS * ndp)
    r_out = Reduce(send, core, along_x, along_z, reduce_refs[0:8], scaling)
    r_uq = Reduce(send, core, along_x, along_z, reduce_refs[8:16], scaling)
    r_vk = Reduce(send, core, along_z, along_x, reduce_refs[16:24], scaling)
    tiles = [slice(t * TILE, (t + 1) * TILE) for t in range(ROWS // TILE)]

    got_x = [
        [send(xg.at[y, rows], xg.at[y, rows], (d, peer)) for _, peer in y_peers]
        for rows in tiles
    ]
    low, high = slice(0, ROWS // 2), slice(ROWS // 2, ROWS)
    pass_up = send(gg.at[y, low], gg.at[y, low], (d, y_up))
    pass_down = send(gg.at[y, high], gg.at[y, high], (d, y_down))
    got_g = [
        send(gg.at[y, high], gg.at[y, high], (d, y_up)),
        send(gg.at[y, low], gg.at[y, low], (d, y_down)),
    ]
    for load in loads[2:]:
        load.wait()
    srow[...] = jnp.broadcast_to(
        start_rows(lens, d * ROWS).astype(jnp.int32), (ROWS, 128)
    )
    wc[y] = wout[:, pl.ds(pl.multiple_of(y * HEAD, HEAD), HEAD)]
    root = 1.0 / math.sqrt(HEAD)

    def attend(scores, begin, width, first, causal):
        scores = scores * root
        col = lax.broadcasted_iota(jnp.int32, scores.shape, 1) + first
        allowed = col >= begin
        if causal is not None:
            row = lax.broadcasted_iota(jnp.int32, scores.shape, 0) + causal
            allowed = allowed & (col <= row)
        sig = 0.5 * jnp.tanh(0.5 * scores) + 0.5
        weight = jnp.where(allowed, scores * sig, 0.0).astype(BF)
        tangent = jnp.where(allowed, sig * (1.0 + scores * (1.0 - sig)) * root, 0.0)
        return weight, tangent

    got_kv = []
    for t, rows in enumerate(tiles):
        for w in got_x[t]:
            w.wait_recv()
        parts = [xg[b, rows].astype(F32) for b in range(NY)]
        mean = column(parts[0] + parts[1] + parts[2] + parts[3]) * (1.0 / WIDTH)
        parts = [part - mean for part in parts]
        var = column(sum(part * part for part in parts)) * (1.0 / WIDTH)
        inv = lax.rsqrt(var + EPSILON)
        xr[rows, :] = jnp.broadcast_to(inv, (TILE, 128))
        for b in range(NY):
            hat = parts[b] * inv
            xh[b, rows] = hat
            xn[rows, b * HEAD : (b + 1) * HEAD] = hat.astype(BF)
        hidden = mm(xn[rows, :], win[...])
        sig = 0.5 * jnp.tanh(0.5 * hidden) + 0.5
        projected = (hidden * sig).astype(BF)
        slopes = sig * (1.0 + hidden * (1.0 - sig))
        for i, g in enumerate((0, 2, 1, 3)):
            cols = slice(g * HEAD, (g + 1) * HEAD)
            proj[i, rows] = projected[:, cols]
            slope[i, rows] = slopes[:, cols]
        got_kv.append(send(proj.at[2:4, rows], kv.at[:, rows], above))
        n = (t + 1) * TILE
        weight, tangent = attend(
            mm(proj[1, rows], proj[3, :n], NT), srow[rows, 0:1], n, 0, t * TILE
        )
        w_own[rows, :n] = weight
        sl_own[rows, :n] = tangent
        att[rows, :] = mm(weight, proj[2, :n])
    got_xn = [send(xn.at[rows], xnp.at[rows], above) for rows in tiles]

    pass_up.wait_recv()
    slot = gg.at[y_down, low]
    got_g.append(send(slot, slot, (d, y_up)))
    pass_down.wait_recv()
    slot = gg.at[y_up, high]
    got_g.append(send(slot, slot, (d, y_down)))
    xnt[:, :ROWS] = xn[...].T

    for t, rows in enumerate(tiles):
        got_kv[t].wait_recv()
        weight, tangent = attend(
            mm(proj[1], kv[1, rows], NT), srow[...], TILE, t * TILE - ROWS, None
        )
        w_prev[:, rows] = weight
        sl_prev[:, rows] = tangent
        att[...] = att[...] + mm(weight, kv[0, rows])

    for w in got_g:
        w.wait_recv()
    d_gated = sum(
        mm(gg[b], wout[:, b * HEAD : (b + 1) * HEAD], NT) for b in range(NY)
    )
    dgate[...] = d_gated
    e = d_gated * proj[0].astype(F32)
    ee[...] = e

    a = att[...]
    sum_a = column(a)
    ca = a - sum_a * (1.0 / HEAD)
    lane = lax.broadcasted_iota(jnp.int32, (ROWS, 128), 1)
    packed = jnp.where(
        lane == 0, sum_a,
        jnp.where(lane == 1, column(ca * ca),
                  jnp.where(lane == 2, column(e), jnp.where(lane == 3, column(e * ca), 0.0))),
    )
    stat[y] = packed.T[:8]
    got_s = [send(stat.at[y], stat.at[y], (d, peer)) for _, peer in y_peers]
    got_w = [
        send(
            wout.at[:, pl.ds(pl.multiple_of(peer * HEAD, HEAD), HEAD)],
            wc.at[y],
            (d, peer),
        )
        for _, peer in y_peers
    ]

    def block_before(t):
        rows = tiles[t]
        got_xn[t].wait_recv()
        for i, g in enumerate((1, 3)):
            hidden = mm(xnp[rows, :], win[:, g * HEAD : (g + 1) * HEAD])
            sig = 0.5 * jnp.tanh(0.5 * hidden) + 0.5
            slope_p[i, rows] = sig * (1.0 + hidden * (1.0 - sig))
        xnt[:, ROWS + t * TILE : ROWS + (t + 1) * TILE] = xnp[rows, :].T

    block_before(0)
    block_before(1)
    for w in got_s:
        w.wait_recv()
    heads = [stat[h] for h in range(NY)]
    mean = sum(h[0:1] for h in heads) * (1.0 / WIDTH)
    var, s_e, s_en = 0.0, 0.0, 0.0
    for h in heads:
        off = h[0:1] * (1.0 / HEAD) - mean
        var = var + h[1:2] + HEAD * off * off
        s_e = s_e + h[2:3]
        s_en = s_en + h[3:4] + off * h[2:3]
    inv = lax.rsqrt(var * (1.0 / WIDTH) + EPSILON)
    line = lax.broadcasted_iota(jnp.int32, (128, ROWS), 0)
    back = jnp.where(
        line == 0, mean,
        jnp.where(line == 1, inv,
                  jnp.where(line == 2, s_e * (1.0 / WIDTH),
                            jnp.where(line == 3, s_en * inv * (1.0 / WIDTH), 0.0))),
    ).T
    mean, inv, s_e, s_en = [back[:, i : i + 1] for i in range(4)]
    normed = (att[...] - mean) * inv
    datt[...] = (inv * (ee[...] - s_e - normed * s_en)).astype(BF)
    gat[y] = (normed * proj[0].astype(F32)).astype(BF)
    dh_uq[0] = (dgate[...] * normed * slope[0]).astype(BF)

    for rows in tiles:
        ds = (mm(datt[rows], kv[0], NT) * sl_prev[rows, :]).astype(BF)
        ds_prev[rows, :] = ds
        dq[rows, :] = mm(ds, kv[1])
    back_v = mm(w_prev[...], datt[...], TN)
    dkv_s[0] = back_v.astype(BF)
    got_dv = send(dkv_s.at[0], dkv_r.at[0], below)
    back_k = mm(ds_prev[...], proj[1], TN)
    dkv_s[1] = back_k.astype(BF)
    got_dk = send(dkv_s.at[1], dkv_r.at[1], below)
    block_before(2)
    block_before(3)
    dh_vk[0, ROWS:] = (back_v * slope_p[0]).astype(BF)
    dh_vk[1, ROWS:] = (back_k * slope_p[1]).astype(BF)
    got_a = [send(gat.at[y], gat.at[y], (d, peer)) for _, peer in y_peers]

    for t, rows in enumerate(tiles):
        n = (t + 1) * TILE
        ds = (mm(datt[rows], proj[2, :n], NT) * sl_own[rows, :n]).astype(BF)
        ds_own[rows, :n] = ds
        dq[rows, :] = dq[rows, :] + mm(ds, proj[3, :n])
    for t, cols in enumerate(tiles):
        dk[cols, :] = mm(ds_own[t * TILE :, cols], proj[1, t * TILE :], TN)
        dv[cols, :] = mm(w_own[t * TILE :, cols], datt[t * TILE :], TN)

    dh_vk[0, :ROWS] = (dv[...] * slope[2]).astype(BF)
    dh_vk[1, :ROWS] = (dk[...] * slope[3]).astype(BF)
    r_vk.s1(mm(xnt[...], dh_vk[1 - c]))
    dh_uq[1] = (dq[...] * slope[1]).astype(BF)
    r_uq.s1(mm(xnt[:, :ROWS], dh_uq[1 - c]))
    gated_t = gat[y].T
    r_out.s1(jnp.concatenate([mm(gated_t, gg[2 * (1 - c) + i]) for i in range(2)], 0))
    r_vk.keep(mm(xnt[...], dh_vk[c]))
    r_vk.s2()
    r_uq.keep(mm(xnt[:, :ROWS], dh_uq[c]))
    r_uq.s2()
    r_out.keep(jnp.concatenate([mm(gated_t, gg[2 * c + i]) for i in range(2)], 0))
    r_out.s2()

    dhid[:, 0:HEAD] = dh_uq[0]
    dhid[:, 2 * HEAD : 3 * HEAD] = dh_uq[1]
    got_dv.wait_recv()
    dhid[:, HEAD : 2 * HEAD] = ((dv[...] + dkv_r[0].astype(F32)) * slope[2]).astype(BF)
    got_dk.wait_recv()
    dhid[:, 3 * HEAD :] = ((dk[...] + dkv_r[1].astype(F32)) * slope[3]).astype(BF)
    one, two = 0.0, 0.0
    for b in range(NY):
        part = mm(dhid[...], win[b * HEAD : (b + 1) * HEAD, :], NT)
        one = one + part
        two = two + part * xh[b]
        din[b] = part
        din_s[b] = part.astype(BF)
    packed = jnp.where(lane == 0, column(one), jnp.where(lane == 1, column(two), 0.0))
    stat2[y] = packed.T[:8]
    got_i = [send(din_s.at[peer], din_r.at[r - 1], (d, peer)) for r, peer in y_peers]
    got_t = [send(stat2.at[y], stat2.at[y], (d, peer)) for _, peer in y_peers]
    r_uq.s3()
    r_vk.s3()
    r_out.s3()

    for w in got_a + got_w:
        w.wait_recv()
    lo[...] = (
        xg[y].astype(F32) + sum(mm(gat[h], wc[h]) for h in range(NY))
    ).astype(BF)

    r_vk.s4()
    r_uq.s4()
    r_out.s4()
    r_vk.s5()
    r_uq.s5()
    r_out.s5()

    for w in got_i + got_t:
        w.wait_recv()
    total = din[y]
    for r in range(NY - 1):
        total = total + din_r[r].astype(F32)
    both = (stat2[0] + stat2[1] + stat2[2] + stat2[3]) * (1.0 / WIDTH)
    back = jnp.where(line == 0, both[0:1], jnp.where(line == 1, both[1:2], 0.0)).T
    piece = xr[:, 0:1] * (total - back[:, 0:1] - xh[y] * back[:, 1:2])
    gt[...] = (gg[y].astype(F32) + piece).astype(BF)

    r_uq.s6()
    r_out.s6()
    r_vk.s6()
    r_uq.s7()
    for i, g in enumerate((0, 2)):
        gwin[:, g * HEAD : (g + 1) * HEAD] = r_uq.full[i].reshape(ROWS, HEAD).astype(F32)
    r_out.s7()
    for b in range(NY):
        block = r_out.full[b // 2, (b % 2) * 2 : (b % 2) * 2 + 2]
        gwout[:, b * HEAD : (b + 1) * HEAD] = block.reshape(HEAD, HEAD)
    r_vk.s7()
    for i, g in enumerate((1, 3)):
        gwin[:, g * HEAD : (g + 1) * HEAD] = r_vk.full[i].reshape(ROWS, HEAD).astype(F32)
    for w in send.copies:
        w.wait_send()


def store(*refs):
    sources, targets, sem = refs[:4], refs[4:8], refs[8]
    copies = [
        pltpu.make_async_copy(src, dst, sem.at[i])
        for i, (src, dst) in enumerate(zip(sources, targets))
    ]
    for copy in copies:
        copy.start()
    for copy in copies:
        copy.wait()


def reduce_scratch(n1, n2, rows, dt):
    block = (n1, n2, rows, HEAD)
    return [
        pltpu.VMEM(block, F32),
        pltpu.VMEM(block, dt),
        pltpu.VMEM(block, dt),
        pltpu.VMEM(block, dt),
        pltpu.VMEM((n1 - 1, n2, rows, HEAD), dt),
        pltpu.VMEM((n2, rows, HEAD), dt),
        pltpu.VMEM((n2 - 1, rows, HEAD), dt),
        pltpu.VMEM((NC,) + block, dt),
    ]


def shards(tokens, lengths, weight_in, weight_out, grad_out):
    lengths = lengths.reshape(1, -1)
    vm = pl.BlockSpec(memory_space=pltpu.VMEM)
    hbm = pl.BlockSpec(memory_space=pltpu.HBM)
    blocks = lambda n, dt: pltpu.VMEM((n, ROWS, HEAD), dt)
    full = lambda dt: pltpu.VMEM((ROWS, WIDTH), dt)
    one = lambda dt: pltpu.VMEM((ROWS, HEAD), dt)
    stats = pltpu.VMEM((NY, 8, ROWS), F32)
    scratch = [
        pltpu.VMEM((1, 128), jnp.int32), full(BF), pltpu.VMEM((HEAD, WIDTH), BF),
        blocks(NY, BF), blocks(NY, BF), pltpu.VMEM((NY, HEAD, HEAD), BF),
        blocks(NY, F32), full(BF), pltpu.VMEM((WIDTH, 2 * ROWS), BF), full(BF), one(F32),
        blocks(4, BF), blocks(4, F32), blocks(2, F32), blocks(2, BF), one(jnp.int32),
        full(BF), full(BF), full(F32), full(F32), full(BF), full(BF),
        stats, blocks(NY, BF), one(F32), one(F32), one(F32), one(BF),
        one(F32), one(F32), one(F32), blocks(2, BF), blocks(2, BF),
        blocks(NY, F32), blocks(NY, BF), blocks(NY - 1, BF), stats,
        full(BF), blocks(2, BF), pltpu.VMEM((2, 2 * ROWS, HEAD), BF),
        *reduce_scratch(NX, NZ, 8, F32),
        *reduce_scratch(NX, NZ, 16, BF),
        *reduce_scratch(NZ, NX, 16, BF),
        pltpu.SemaphoreType.DMA((5,)),
        pltpu.SemaphoreType.DMA((160,)),
        pltpu.SemaphoreType.DMA((160,)),
    ]
    shapes = (
        jax.ShapeDtypeStruct((ROWS, HEAD), BF),
        jax.ShapeDtypeStruct((ROWS, HEAD), BF),
        jax.ShapeDtypeStruct((WIDTH, 4 * HEAD), F32),
        jax.ShapeDtypeStruct((HEAD, WIDTH), F32),
    )
    results = pl.pallas_call(
        kernel,
        out_shape=shapes,
        in_specs=[hbm] * 5,
        out_specs=(vm,) * 4,
        scratch_shapes=scratch,
        compiler_params=pltpu.CompilerParams(
            collective_id=0, has_side_effects=True, vmem_limit_bytes=62 * 1024 * 1024
        ),
        name="layer",
    )(tokens, lengths, weight_in, weight_out, grad_out)
    return pl.pallas_call(
        store,
        out_shape=shapes,
        in_specs=[vm] * 4,
        out_specs=(hbm,) * 4,
        scratch_shapes=[pltpu.SemaphoreType.DMA((4,))],
        name="store",
    )(*results)


def solution(mesh):
    placed = (P("dp", "sub"), P(), P(None, "sub"), P("sub", None), P("dp", "sub"))
    return jax.shard_map(
        shards,
        mesh=mesh,
        in_specs=placed,
        out_specs=(P("dp", "sub"), P("dp", "sub"), P(None, "sub"), P("sub", None)),
        check_vma=False,
    )
```

```python
import functools
import math

import jax
import jax.numpy as jnp
from jax import lax
from jax.experimental import pallas as pl
from jax.experimental.pallas import tpu as pltpu
from jax.sharding import PartitionSpec as P

EPSILON = 1e-05
NX, NZ, NC, NY = 4, 8, 2, 4
ROWS, HEAD, WIDTH = 512, 128, 512
TILE = 128
MESH = pl.DeviceIdType.MESH
BF, F32 = jnp.bfloat16, jnp.float32

NN = (((1,), (0,)), ((), ()))
NT = (((1,), (1,)), ((), ()))
TN = (((0,), (0,)), ((), ()))


def mm(left, right, dims=NN):
    return lax.dot_general(left, right, dims, preferred_element_type=F32)


class Copy:
    def __init__(self, copy):
        self.copy, self.left, self.landed = copy, False, False
        copy.start()

    def wait_recv(self):
        if not self.landed:
            self.copy.wait_recv()
        self.landed = True

    def wait_send(self):
        if not self.left:
            self.copy.wait_send()
        self.left = True


class Sender:
    def __init__(self, send_sem, recv_sem):
        self.send_sem, self.recv_sem, self.copies = send_sem, recv_sem, []

    def __call__(self, src, dst, device):
        i = len(self.copies)
        copy = Copy(
            pltpu.make_async_remote_copy(
                src_ref=src,
                dst_ref=dst,
                send_sem=self.send_sem.at[i],
                recv_sem=self.recv_sem.at[i],
                device_id=device,
                device_id_type=MESH,
            )
        )
        self.copies.append(copy)
        return copy


def far_first(n):
    return sorted(range(1, n), key=lambda r: (-min(r, n - r), r))


class Reduce:
    def __init__(self, send, core, first, second, refs, scale):
        self.send, self.scale = send, scale
        self.c, self.core = core
        self.n1, self.i1, self.at1 = first
        self.n2, self.i2, self.at2 = second
        self.part, self.sb, self.rc, self.s_1, self.r_1, self.s_2, self.r_2, self.full = refs
        self.dt = self.full.dtype

    def to1(self, r):
        return lax.rem(self.i1 + r, self.n1)

    def to2(self, r):
        return lax.rem(self.i2 + r, self.n2)

    def s1(self, other):
        self.sb[...] = other.astype(self.dt).reshape(self.sb.shape)
        self.w1 = self.send(self.sb, self.rc, self.core)

    def keep(self, own):
        self.part[...] = own.reshape(self.part.shape)

    def s2(self):
        self.w1.wait_recv()
        total = self.part[...] + self.rc[...].astype(F32)
        self.part[...] = total
        self.s_1[...] = total.astype(self.dt)
        self.w2 = []
        for r in far_first(self.n1):
            to = self.to1(r)
            self.w2.append(self.send(self.s_1.at[to], self.r_1.at[r - 1], self.at1(to)))

    def s3(self):
        for w in self.w2:
            w.wait_recv()
        total = self.part[self.i1]
        for r in range(self.n1 - 1):
            total = total + self.r_1[r].astype(F32)
        self.part[0] = total
        self.s_2[...] = total.astype(self.dt)
        self.w3 = []
        for r in far_first(self.n2):
            to = self.to2(r)
            self.w3.append(self.send(self.s_2.at[to], self.r_2.at[r - 1], self.at2(to)))

    def s4(self):
        for w in self.w3:
            w.wait_recv()
        total = self.part[0, self.i2]
        for r in range(self.n2 - 1):
            total = total + self.r_2[r].astype(F32)
        mine = self.full.at[self.c, self.i1, self.i2]
        self.full[self.c, self.i1, self.i2] = (total * self.scale).astype(self.dt)
        self.w4 = [
            self.send(mine, mine, self.at2(self.to2(r))) for r in far_first(self.n2)
        ]

    def s5(self):
        for w in self.w4:
            w.wait_recv()
        mine = self.full.at[self.c, self.i1]
        self.w5 = [
            (r, self.send(mine, mine, self.at1(self.to1(r)))) for r in far_first(self.n1)
        ]
        self.w6 = [self.send(mine, mine, self.core)]

    def s6(self):
        for r, w in self.w5[::-1]:
            w.wait_recv()
            piece = self.full.at[self.c, lax.rem(self.i1 + self.n1 - r, self.n1)]
            self.w6.append(self.send(piece, piece, self.core))

    def s7(self):
        for w in self.w6:
            w.wait_recv()


class Reduce3:
    def __init__(self, send, core, first, second, refs, scale):
        self.send, self.scale = send, scale
        self.c, self.core = core
        self.n1, self.i1, self.at1 = first
        self.n2, self.i2, self.at2 = second
        self.part, self.sb, self.rc, self.s_1, self.r_1, self.both, self.full = refs
        self.dt = self.full.dtype

    def s1(self, other):
        self.sb[...] = other.astype(self.dt).reshape(self.sb.shape)
        self.w1 = self.send(self.sb, self.rc, self.core)

    def keep(self, own):
        self.part[...] = own.reshape(self.part.shape)

    def s2(self):
        self.w1.wait_recv()
        total = self.part[...] + self.rc[...].astype(F32)
        self.part[...] = total
        self.s_1[...] = total.astype(self.dt)
        self.w2 = []
        for r in far_first(self.n1):
            to = lax.rem(self.i1 + r, self.n1)
            self.w2.append(self.send(self.s_1.at[to], self.r_1.at[r - 1], self.at1(to)))

    def s3(self):
        for w in self.w2:
            w.wait_recv()
        total = self.part[self.i1]
        for r in range(self.n1 - 1):
            total = total + self.r_1[r].astype(F32)
        self.both[self.i2] = total.astype(self.dt)
        mine = self.both.at[self.i2]
        self.w3 = [
            self.send(mine, mine, self.at2(lax.rem(self.i2 + r, self.n2)))
            for r in far_first(self.n2)
        ]

    def s4(self):
        for w in self.w3:
            w.wait_recv()
        total = self.both[0].astype(F32)
        for k in range(1, self.n2):
            total = total + self.both[k].astype(F32)
        self.full[self.c, self.i1] = (total * self.scale).astype(self.dt)
        mine = self.full.at[self.c, self.i1]
        self.w4 = [
            (r, self.send(mine, mine, self.at1(lax.rem(self.i1 + r, self.n1))))
            for r in far_first(self.n1)
        ]
        self.w5 = [self.send(mine, mine, self.core)]

    def s5(self):
        for r, w in self.w4[::-1]:
            w.wait_recv()
            piece = self.full.at[self.c, lax.rem(self.i1 + self.n1 - r, self.n1)]
            self.w5.append(self.send(piece, piece, self.core))

    def s6(self):
        for w in self.w5:
            w.wait_recv()


def column(value):
    return jnp.sum(value, axis=1, keepdims=True)


def start_rows(lens_ref, first_row):
    lens = jnp.broadcast_to(lens_ref[...].astype(F32), (128, 128))
    down = lax.broadcasted_iota(jnp.int32, (128, 128), 0)
    across = lax.broadcasted_iota(jnp.int32, (128, 128), 1)
    as_column = column(jnp.where(down == across, lens, 0.0))
    starts = jnp.sum(jnp.where(down < across, as_column, 0.0), axis=0, keepdims=True)
    rows = (first_row + lax.broadcasted_iota(jnp.int32, (ROWS, 128), 0)).astype(F32)
    own = jnp.max(jnp.where(starts <= rows, starts, 0.0), axis=1, keepdims=True)
    return own - first_row.astype(F32)


def kernel(
    tok_h, len_h, win_h, wout_h, gout_h,
    lo, gt, gwin, gwout,
    lens, win, wout, lo_v, gt_v, gwin_v, gwout_v,
    xg, gg, wc, xh, xn, xnt, xnp, xr, gate, qb, kv, slope, slope_p, srow,
    wt, sl, slt, wp,
    stat, gat, att, ee, dgate, datt, ds, dk, dv, dkv_s, dkv_r,
    din, din_s, din_r, stat2, dhid, dh_u, dh_q, dh_vk, pair,
    *rest,
):
    reduce_refs, (load_sem, out_sem, send_sem, recv_sem) = rest[:-4], rest[-4:]
    d, y = lax.axis_index("dp"), lax.axis_index("sub")
    c = lax.rem(d, NC)
    z = lax.rem(d // NC, NZ)
    x = d // (NC * NZ)
    ndp = NX * NZ * NC

    def at(ax, az, ac):
        return ((ax * NZ + az) * NC + ac, y)

    above = (lax.rem(d + 1, ndp), y)
    below = (lax.rem(d + ndp - 1, ndp), y)
    y_peers = [(r, lax.rem(y + r, NY)) for r in (2, 1, 3)]
    y_up, y_down = lax.rem(y + 1, NY), lax.rem(y + NY - 1, NY)

    loads = [
        pltpu.make_async_copy(src, dst, load_sem.at[i])
        for i, (src, dst) in enumerate(
            [
                (tok_h, xg.at[y]), (gout_h, gg.at[y]), (len_h, lens),
                (win_h, win), (wout_h, wout),
            ]
        )
    ]
    for load in loads:
        load.start()
    stores = []

    def put(src, dst):
        copy = pltpu.make_async_copy(src, dst, out_sem.at[len(stores)])
        copy.start()
        stores.append(copy)

    barrier = pltpu.get_barrier_semaphore()
    greet = [(d, peer) for _, peer in y_peers]
    greet += [at(lax.rem(x + r, NX), z, c) for r in range(1, NX)]
    greet += [at(x, lax.rem(z + r, NZ), c) for r in range(1, NZ)]
    greet += [at(x, z, 1 - c)]
    greet += [(lax.rem(d + ndp + 2 * c - 1, ndp), y)]
    for device in greet:
        pl.semaphore_signal(barrier, inc=1, device_id=device, device_id_type=MESH)
    for load in loads:
        load.wait()
    pl.semaphore_wait(barrier, len(greet))

    send = Sender(send_sem, recv_sem)
    core = (c, at(x, z, 1 - c))
    along_x = (NX, x, lambda to: at(to, z, c))
    along_z = (NZ, z, lambda to: at(x, to, c))
    scaling = 1.0 / math.sqrt(ROWS * ndp)
    r_uo = Reduce(send, core, along_x, along_z, reduce_refs[0:8], scaling)
    r_vk = Reduce3(send, core, along_z, along_x, reduce_refs[8:15], scaling)
    r_q = Reduce3(send, core, along_z, along_x, reduce_refs[15:22], scaling)
    tiles = [slice(t * TILE, (t + 1) * TILE) for t in range(ROWS // TILE)]
    half = ROWS // 2
    low, high = slice(0, half), slice(half, ROWS)

    got_x = []
    for rows in tiles:
        got_x.append([send(xg.at[y, rows], xg.at[y, rows], (d, peer)) for _, peer in y_peers])
    pass_up = send(gg.at[y, low], gg.at[y, low], (d, y_up))
    pass_down = send(gg.at[y, high], gg.at[y, high], (d, y_down))
    got_g = [
        send(gg.at[y, high], gg.at[y, high], (d, y_up)),
        send(gg.at[y, low], gg.at[y, low], (d, y_down)),
    ]
    srow[...] = jnp.broadcast_to(
        start_rows(lens, d * ROWS).astype(jnp.int32), (ROWS, 128)
    )
    wc[y] = wout[:, pl.ds(pl.multiple_of(y * HEAD, HEAD), HEAD)]
    root = 1.0 / math.sqrt(HEAD)

    def attend(scores, begin, first, causal):
        scores = scores * root
        col = lax.broadcasted_iota(jnp.int32, scores.shape, 1) + first
        allowed = col >= begin
        if causal is not None:
            row = lax.broadcasted_iota(jnp.int32, scores.shape, 0) + causal
            allowed = allowed & (col <= row)
        sig = 0.5 * jnp.tanh(0.5 * scores) + 0.5
        weight = jnp.where(allowed, scores * sig, 0.0).astype(BF)
        tangent = jnp.where(allowed, sig * (1.0 + scores * (1.0 - sig)) * root, 0.0)
        return weight, tangent

    got_kv = []
    for t, rows in enumerate(tiles):
        for w in got_x[t]:
            w.wait_recv()
        parts = [xg[b, rows].astype(F32) for b in range(NY)]
        mean = column(parts[0] + parts[1] + parts[2] + parts[3]) * (1.0 / WIDTH)
        parts = [part - mean for part in parts]
        var = column(sum(part * part for part in parts)) * (1.0 / WIDTH)
        inv = lax.rsqrt(var + EPSILON)
        xr[rows, :] = jnp.broadcast_to(inv, (TILE, 128))
        for b in range(NY):
            hat = parts[b] * inv
            xh[b, rows] = hat
            xn[rows, b * HEAD : (b + 1) * HEAD] = hat.astype(BF)
        hidden = mm(xn[rows, :], win[...])
        sig = 0.5 * jnp.tanh(0.5 * hidden) + 0.5
        projected = (hidden * sig).astype(BF)
        own = slice(ROWS + t * TILE, ROWS + (t + 1) * TILE)
        kv[0, own] = projected[:, HEAD : 2 * HEAD]
        kv[1, own] = projected[:, 3 * HEAD :]
        got_kv.append(send(kv.at[:, own], kv.at[:, rows], above))
        gate[rows, :] = projected[:, :HEAD]
        qb[rows, :] = projected[:, 2 * HEAD : 3 * HEAD]
        slopes = sig * (1.0 + hidden * (1.0 - sig))
        for i, g in enumerate((0, 2, 1, 3)):
            slope[i, rows] = slopes[:, g * HEAD : (g + 1) * HEAD]

    pass_up.wait_recv()
    slot = gg.at[y_down, low]
    got_g.append(send(slot, slot, (d, y_up)))
    pass_down.wait_recv()
    slot = gg.at[y_up, high]
    got_g.append(send(slot, slot, (d, y_down)))

    for t, rows in enumerate(tiles):
        weight, tangent = attend(
            mm(qb[rows, :], kv[1, ROWS:], NT), srow[rows, 0:1], 0, t * TILE
        )
        wt[ROWS:, rows] = weight.T
        sl[rows, ROWS:] = tangent
        slt[ROWS:, rows] = tangent.T
        att[rows, :] = mm(weight, kv[0, ROWS:])
    got_xn = [send(xn.at[rows], xnp.at[rows], above) for rows in (low, high)]
    xnt[:, ROWS:] = xn[...].T

    for t, cols in enumerate(tiles):
        got_kv[t].wait_recv()
        weight, tangent = attend(
            mm(qb[...], kv[1, cols], NT), srow[...], t * TILE - ROWS, None
        )
        wp[:, cols] = weight
        sl[:, cols] = tangent
        att[...] = att[...] + mm(weight, kv[0, cols])

    for w in got_g:
        w.wait_recv()
    d_gated = sum(
        mm(gg[b], wout[:, b * HEAD : (b + 1) * HEAD], NT) for b in range(NY)
    )
    dgate[...] = d_gated
    e = d_gated * gate[...].astype(F32)
    ee[...] = e

    a = att[...]
    sum_a = column(a)
    ca = a - sum_a * (1.0 / HEAD)
    lane = lax.broadcasted_iota(jnp.int32, (ROWS, 128), 1)
    packed = jnp.where(
        lane == 0, sum_a,
        jnp.where(lane == 1, column(ca * ca),
                  jnp.where(lane == 2, column(e), jnp.where(lane == 3, column(e * ca), 0.0))),
    )
    stat[y] = packed.T[:8]
    got_s = [send(stat.at[y], stat.at[y], (d, peer)) for _, peer in y_peers]
    for rows in tiles:
        wt[rows, :] = wp[:, rows].T
        slt[rows, :] = sl[:, rows].T
    for w in got_s:
        w.wait_recv()
    heads = [stat[h] for h in range(NY)]
    mean = sum(h[0:1] for h in heads) * (1.0 / WIDTH)
    var, s_e, s_en = 0.0, 0.0, 0.0
    for h in heads:
        off = h[0:1] * (1.0 / HEAD) - mean
        var = var + h[1:2] + HEAD * off * off
        s_e = s_e + h[2:3]
        s_en = s_en + h[3:4] + off * h[2:3]
    inv = lax.rsqrt(var * (1.0 / WIDTH) + EPSILON)
    line = lax.broadcasted_iota(jnp.int32, (128, ROWS), 0)
    back = jnp.where(
        line == 0, mean,
        jnp.where(line == 1, inv,
                  jnp.where(line == 2, s_e * (1.0 / WIDTH),
                            jnp.where(line == 3, s_en * inv * (1.0 / WIDTH), 0.0))),
    ).T
    mean, inv, s_e, s_en = [back[:, i : i + 1] for i in range(4)]
    normed = (att[...] - mean) * inv
    datt[...] = (inv * (ee[...] - s_e - normed * s_en)).astype(BF)
    gat[y] = (normed * gate[...].astype(F32)).astype(BF)
    got_a = [send(gat.at[y], gat.at[y], (d, peer)) for _, peer in y_peers]
    got_w = [
        send(
            wout.at[:, pl.ds(pl.multiple_of(peer * HEAD, HEAD), HEAD)],
            wc.at[y],
            (d, peer),
        )
        for _, peer in y_peers
    ]
    dh_u[...] = (dgate[...] * normed * slope[0]).astype(BF)

    gated_t = gat[y].T
    pair[0] = mm(xnt[:, ROWS:], dh_u[...])
    for b in range(NY):
        pair[1, b * HEAD : (b + 1) * HEAD] = mm(gated_t, gg[b])
    r_uo.s1(pair[1 - c])
    r_uo.keep(pair[c])

    def key_grads(rows):
        d_st = (mm(kv[0, rows], datt[...], NT) * slt[rows, :]).astype(BF)
        dk[rows, :] = mm(d_st, qb[...])
        dv[rows, :] = mm(wt[rows, :], datt[...])

    for t in range(ROWS // TILE):
        key_grads(tiles[t])
    dkv_s[0] = dv[:ROWS, :].astype(BF)
    dkv_s[1] = dk[:ROWS, :].astype(BF)
    got_dkv = send(dkv_s, dkv_r, below)
    for t in range(ROWS // TILE):
        key_grads(slice(ROWS + t * TILE, ROWS + (t + 1) * TILE))
    r_uo.s2()

    for t, rows in enumerate((low, high)):
        got_xn[t].wait_recv()
        for i, g in enumerate((1, 3)):
            hidden = mm(xnp[rows, :], win[:, g * HEAD : (g + 1) * HEAD])
            sig = 0.5 * jnp.tanh(0.5 * hidden) + 0.5
            slope_p[i, rows] = sig * (1.0 + hidden * (1.0 - sig))
        xnt[:, rows] = xnp[rows, :].T
    dh_vk[:ROWS, :HEAD] = (dv[:ROWS, :] * slope_p[0]).astype(BF)
    dh_vk[:ROWS, HEAD:] = (dk[:ROWS, :] * slope_p[1]).astype(BF)
    dh_vk[ROWS:, :HEAD] = (dv[ROWS:, :] * slope[2]).astype(BF)
    dh_vk[ROWS:, HEAD:] = (dk[ROWS:, :] * slope[3]).astype(BF)
    mine = pl.ds(pl.multiple_of(c * half, half), half)
    theirs = pl.ds(pl.multiple_of((1 - c) * half, half), half)
    r_vk.s1(mm(xnt[theirs, :], dh_vk[...]))

    for rows in tiles:
        ds[rows, :] = (mm(datt[rows, :], kv[0], NT) * sl[rows, :]).astype(BF)
        dq = mm(ds[rows, :], kv[1])
        dh_q[rows, :] = (dq * slope[1, rows]).astype(BF)
    r_q.s1(mm(xnt[theirs, ROWS:], dh_q[...]))
    r_vk.keep(mm(xnt[mine, :], dh_vk[...]))
    r_vk.s2()
    r_q.keep(mm(xnt[mine, ROWS:], dh_q[...]))
    r_q.s2()
    r_uo.s3()

    dhid[:, 0:HEAD] = dh_u[...]
    dhid[:, 2 * HEAD : 3 * HEAD] = dh_q[...]
    got_dkv.wait_recv()
    dhid[:, HEAD : 2 * HEAD] = ((dv[ROWS:, :] + dkv_r[0].astype(F32)) * slope[2]).astype(BF)
    dhid[:, 3 * HEAD :] = ((dk[ROWS:, :] + dkv_r[1].astype(F32)) * slope[3]).astype(BF)
    one, two = 0.0, 0.0
    for b in range(NY):
        part = mm(dhid[...], win[b * HEAD : (b + 1) * HEAD, :], NT)
        one = one + part
        two = two + part * xh[b]
        din[b] = part
        din_s[b] = part.astype(BF)
    packed = jnp.where(lane == 0, column(one), jnp.where(lane == 1, column(two), 0.0))
    stat2[y] = packed.T[:8]
    got_i = [send(din_s.at[peer], din_r.at[r - 1], (d, peer)) for r, peer in y_peers]
    got_t = [send(stat2.at[y], stat2.at[y], (d, peer)) for _, peer in y_peers]
    for w in got_a + got_w:
        w.wait_recv()
    lo_v[...] = (
        xg[y].astype(F32) + sum(mm(gat[h], wc[h]) for h in range(NY))
    ).astype(BF)
    put(lo_v, lo)
    r_vk.s3()
    r_q.s3()
    r_uo.s4()
    r_vk.s4()
    r_q.s4()
    r_uo.s5()

    for w in got_i + got_t:
        w.wait_recv()
    total = din[y]
    for r in range(NY - 1):
        total = total + din_r[r].astype(F32)
    both = (stat2[0] + stat2[1] + stat2[2] + stat2[3]) * (1.0 / WIDTH)
    back = jnp.where(line == 0, both[0:1], jnp.where(line == 1, both[1:2], 0.0)).T
    piece = xr[:, 0:1] * (total - back[:, 0:1] - xh[y] * back[:, 1:2])
    gt_v[...] = (gg[y].astype(F32) + piece).astype(BF)
    put(gt_v, gt)

    def put_columns(g, value):
        cols = slice(g * HEAD, (g + 1) * HEAD)
        gwin_v[:, cols] = value.astype(F32)
        put(gwin_v.at[:, cols], gwin.at[:, cols])

    r_vk.s5()
    r_q.s5()
    r_uo.s6()
    r_vk.s6()
    done = r_vk.full[...].reshape(ROWS, 2 * HEAD)
    put_columns(1, done[:, :HEAD])
    put_columns(3, done[:, HEAD:])
    r_q.s6()
    put_columns(2, r_q.full[...].reshape(ROWS, HEAD))
    r_uo.s7()
    put_columns(0, r_uo.full[0].reshape(ROWS, HEAD))
    for b in range(NY):
        gwout_v[:, b * HEAD : (b + 1) * HEAD] = r_uo.full[1, b].reshape(HEAD, HEAD).astype(F32)
    put(gwout_v, gwout)
    for w in send.copies:
        w.wait_send()
    for w in stores:
        w.wait()


def store(*refs):
    sources, targets, stages, sems = refs[:4], refs[4:8], refs[8:12], refs[12:]
    parts = [(i, slice(None)) for i in (0, 1, 3)]
    parts += [(2, slice(t * TILE, (t + 1) * TILE)) for t in range(WIDTH // TILE)]
    reads, writes = [], []
    for n, (i, rows) in enumerate(parts):
        stage = stages[i].at[rows]
        reads.append(pltpu.make_async_copy(sources[i].at[rows], stage, sems[0].at[n]))
        writes.append(pltpu.make_async_copy(stage, targets[i].at[rows], sems[1].at[n]))
    for read in reads:
        read.start()
    for read, write in zip(reads, writes):
        read.wait()
        write.start()
    for write in writes:
        write.wait()


def reduce3_scratch(n):
    r = ROWS // (NC * NZ)
    block = (NZ, r, n)
    return [
        pltpu.VMEM(block, F32),
        pltpu.VMEM(block, BF),
        pltpu.VMEM(block, BF),
        pltpu.VMEM(block, BF),
        pltpu.VMEM((NZ - 1, r, n), BF),
        pltpu.VMEM((NX, r, n), BF),
        pltpu.VMEM((NC,) + block, BF),
    ]


def reduce_scratch(n1, n2, rows, dt):
    block = (n1, n2, rows, HEAD)
    return [
        pltpu.VMEM(block, F32),
        pltpu.VMEM(block, dt),
        pltpu.VMEM(block, dt),
        pltpu.VMEM(block, dt),
        pltpu.VMEM((n1 - 1, n2, rows, HEAD), dt),
        pltpu.VMEM((n2, rows, HEAD), dt),
        pltpu.VMEM((n2 - 1, rows, HEAD), dt),
        pltpu.VMEM((NC,) + block, dt),
    ]


def shards(tokens, lengths, weight_in, weight_out, grad_out):
    lengths = lengths.reshape(1, -1)
    hbm = pl.BlockSpec(memory_space=pltpu.HBM)
    blocks = lambda n, dt: pltpu.VMEM((n, ROWS, HEAD), dt)
    full = lambda dt: pltpu.VMEM((ROWS, WIDTH), dt)
    one = lambda dt: pltpu.VMEM((ROWS, HEAD), dt)
    tall = lambda n, dt: pltpu.VMEM((2 * ROWS, n), dt)
    stats = pltpu.VMEM((NY, 8, ROWS), F32)
    scratch = [
        pltpu.VMEM((1, 128), jnp.int32), full(BF), pltpu.VMEM((HEAD, WIDTH), BF),
        one(BF), one(BF), full(F32), pltpu.VMEM((HEAD, WIDTH), F32),
        blocks(NY, BF), blocks(NY, BF), pltpu.VMEM((NY, HEAD, HEAD), BF),
        blocks(NY, F32), full(BF), pltpu.VMEM((WIDTH, 2 * ROWS), BF), full(BF), one(F32),
        one(BF), one(BF), pltpu.VMEM((2, 2 * ROWS, HEAD), BF), blocks(4, F32),
        blocks(2, F32), one(jnp.int32),
        tall(ROWS, BF), pltpu.VMEM((ROWS, 2 * ROWS), F32), tall(ROWS, F32), full(BF),
        stats, blocks(NY, BF), one(F32), one(F32), one(F32), one(BF),
        pltpu.VMEM((ROWS, 2 * ROWS), BF), tall(HEAD, F32), tall(HEAD, F32),
        blocks(2, BF), blocks(2, BF),
        blocks(NY, F32), blocks(NY, BF), blocks(NY - 1, BF), stats,
        full(BF), one(BF), one(BF), tall(2 * HEAD, BF), blocks(2, F32),
        *reduce_scratch(NX, NZ, 16, BF),
        *reduce3_scratch(2 * HEAD),
        *reduce3_scratch(HEAD),
        pltpu.SemaphoreType.DMA((5,)),
        pltpu.SemaphoreType.DMA((8,)),
        pltpu.SemaphoreType.DMA((160,)),
        pltpu.SemaphoreType.DMA((160,)),
    ]
    shapes = (
        jax.ShapeDtypeStruct((ROWS, HEAD), BF),
        jax.ShapeDtypeStruct((ROWS, HEAD), BF),
        jax.ShapeDtypeStruct((WIDTH, 4 * HEAD), F32),
        jax.ShapeDtypeStruct((HEAD, WIDTH), F32),
    )
    results = pl.pallas_call(
        kernel,
        out_shape=shapes,
        in_specs=[hbm] * 5,
        out_specs=(hbm,) * 4,
        scratch_shapes=scratch,
        compiler_params=pltpu.CompilerParams(
            collective_id=0, has_side_effects=True, vmem_limit_bytes=62 * 1024 * 1024
        ),
        name="layer",
    )(tokens, lengths, weight_in, weight_out, grad_out)
    return pl.pallas_call(
        store,
        out_shape=shapes,
        in_specs=[hbm] * 4,
        out_specs=(hbm,) * 4,
        scratch_shapes=[pltpu.VMEM(shape.shape, shape.dtype) for shape in shapes]
        + [pltpu.SemaphoreType.DMA((7,))] * 2,
        name="store",
    )(*results)


def solution(mesh):
    placed = (P("dp", "sub"), P(), P(None, "sub"), P("sub", None), P("dp", "sub"))
    return jax.shard_map(
        shards,
        mesh=mesh,
        in_specs=placed,
        out_specs=(P("dp", "sub"), P("dp", "sub"), P(None, "sub"), P("sub", None)),
        check_vma=False,
    )
```

```python
import functools
import math

import jax
import jax.numpy as jnp
from jax import lax
from jax.experimental import pallas as pl
from jax.experimental.pallas import tpu as pltpu
from jax.sharding import PartitionSpec as P

EPSILON = 1e-05
NX, NZ, NC, NY = 4, 8, 2, 4
ROWS, HEAD, WIDTH = 512, 128, 512
TILE = 128
MESH = pl.DeviceIdType.MESH
BF, F32 = jnp.bfloat16, jnp.float32

NN = (((1,), (0,)), ((), ()))
NT = (((1,), (1,)), ((), ()))
TN = (((0,), (0,)), ((), ()))


def mm(left, right, dims=NN):
    return lax.dot_general(left, right, dims, preferred_element_type=F32)


class Exchange:
    def __init__(self, make, whole):
        self.make, self.whole = make, whole

    def add(self, src, dst, device):
        self.make(src, dst, device).start()
        self.device = device
        return self

    def wait_recv(self):
        self.make(self.whole, self.whole, self.device).wait_recv()

    def wait_send(self):
        self.make(self.whole, self.whole, self.device).wait_send()


class Sender:
    def __init__(self, send_sem, recv_sem):
        self.send_sem, self.recv_sem, self.groups = send_sem, recv_sem, []

    def group(self, whole, copies=()):
        i = len(self.groups)

        def make(src, dst, device):
            return pltpu.make_async_remote_copy(
                src_ref=src,
                dst_ref=dst,
                send_sem=self.send_sem.at[i],
                recv_sem=self.recv_sem.at[i],
                device_id=device,
                device_id_type=MESH,
            )

        group = Exchange(make, whole)
        self.groups.append(group)
        for src, dst, device in copies:
            group.add(src, dst, device)
        return group

    def __call__(self, src, dst, device):
        return self.group(src, [(src, dst, device)])


def far_first(n):
    return sorted(range(1, n), key=lambda r: (-min(r, n - r), r))


class Reduce:
    def __init__(self, send, core, first, second, refs, scale):
        self.send, self.scale = send, scale
        self.c, self.core = core
        self.n1, self.i1, self.at1 = first
        self.n2, self.i2, self.at2 = second
        self.part, self.sb, self.rc, self.s_1, self.r_1, self.s_2, self.r_2, self.full = refs
        self.dt = self.full.dtype

    def to1(self, r):
        return lax.rem(self.i1 + r, self.n1)

    def to2(self, r):
        return lax.rem(self.i2 + r, self.n2)

    def s1(self, other):
        self.sb[...] = other.astype(self.dt).reshape(self.sb.shape)
        self.w1 = self.send(self.sb, self.rc, self.core)

    def keep(self, own):
        self.part[...] = own.reshape(self.part.shape)

    def s2(self):
        self.w1.wait_recv()
        total = self.part[...] + self.rc[...].astype(F32)
        self.part[...] = total
        self.s_1[...] = total.astype(self.dt)
        self.w2 = self.send.group(self.r_1)
        for r in far_first(self.n1):
            to = self.to1(r)
            self.w2.add(self.s_1.at[to], self.r_1.at[r - 1], self.at1(to))

    def s3(self):
        self.w2.wait_recv()
        total = self.part[self.i1]
        for r in range(self.n1 - 1):
            total = total + self.r_1[r].astype(F32)
        self.part[0] = total
        self.s_2[...] = total.astype(self.dt)
        self.w3 = self.send.group(self.r_2)
        for r in far_first(self.n2):
            to = self.to2(r)
            self.w3.add(self.s_2.at[to], self.r_2.at[r - 1], self.at2(to))

    def s4(self):
        self.w3.wait_recv()
        total = self.part[0, self.i2]
        for r in range(self.n2 - 1):
            total = total + self.r_2[r].astype(F32)
        mine = self.full.at[self.c, self.i1, self.i2]
        self.full[self.c, self.i1, self.i2] = (total * self.scale).astype(self.dt)
        self.w4 = self.send.group(
            self.r_2, [(mine, mine, self.at2(self.to2(r))) for r in far_first(self.n2)]
        )

    def s5(self):
        self.w4.wait_recv()
        mine = self.full.at[self.c, self.i1]
        self.w5 = [
            (r, self.send(mine, mine, self.at1(self.to1(r)))) for r in far_first(self.n1)
        ]
        self.w6 = self.send.group(self.s_1, [(mine, mine, self.core)])

    def s6(self):
        for r, w in self.w5[::-1]:
            w.wait_recv()
            piece = self.full.at[self.c, lax.rem(self.i1 + self.n1 - r, self.n1)]
            self.w6.add(piece, piece, self.core)

    def s7(self):
        self.w6.wait_recv()


class Reduce3:
    def __init__(self, send, core, first, second, refs, scale):
        self.send, self.scale = send, scale
        self.c, self.core = core
        self.n1, self.i1, self.at1 = first
        self.n2, self.i2, self.at2 = second
        self.part, self.sb, self.rc, self.s_1, self.r_1, self.both, self.full = refs
        self.dt = self.full.dtype

    def s1(self, other):
        self.sb[...] = other.astype(self.dt).reshape(self.sb.shape)
        self.w1 = self.send(self.sb, self.rc, self.core)

    def keep(self, own):
        self.part[...] = own.reshape(self.part.shape)

    def s2(self):
        self.w1.wait_recv()
        total = self.part[...] + self.rc[...].astype(F32)
        self.part[...] = total
        self.s_1[...] = total.astype(self.dt)
        self.w2 = self.send.group(self.r_1)
        for r in far_first(self.n1):
            to = lax.rem(self.i1 + r, self.n1)
            self.w2.add(self.s_1.at[to], self.r_1.at[r - 1], self.at1(to))

    def s3(self):
        self.w2.wait_recv()
        total = self.part[self.i1]
        for r in range(self.n1 - 1):
            total = total + self.r_1[r].astype(F32)
        self.both[self.i2] = total.astype(self.dt)
        mine = self.both.at[self.i2]
        self.w3 = self.send.group(
            self.both.at[0 : self.n2 - 1],
            [
                (mine, mine, self.at2(lax.rem(self.i2 + r, self.n2)))
                for r in far_first(self.n2)
            ],
        )

    def s4(self):
        self.w3.wait_recv()
        total = self.both[0].astype(F32)
        for k in range(1, self.n2):
            total = total + self.both[k].astype(F32)
        self.full[self.c, self.i1] = (total * self.scale).astype(self.dt)
        mine = self.full.at[self.c, self.i1]
        order = far_first(self.n1)
        self.w4 = []
        for steps in (order[:3], order[3:]):
            peers = [self.at1(lax.rem(self.i1 + r, self.n1)) for r in steps]
            whole = self.r_1.at[0 : len(steps)]
            self.w4.append((steps, self.send.group(whole, [(mine, mine, to) for to in peers])))
        self.w5 = self.send.group(self.s_1, [(mine, mine, self.core)])

    def s5(self):
        for steps, w in self.w4[::-1]:
            w.wait_recv()
            for r in steps:
                piece = self.full.at[self.c, lax.rem(self.i1 + self.n1 - r, self.n1)]
                self.w5.add(piece, piece, self.core)

    def s6(self):
        self.w5.wait_recv()


def column(value):
    return jnp.sum(value, axis=1, keepdims=True)


def start_rows(lens_ref, first_row):
    lens = jnp.broadcast_to(lens_ref[...].astype(F32), (128, 128))
    down = lax.broadcasted_iota(jnp.int32, (128, 128), 0)
    across = lax.broadcasted_iota(jnp.int32, (128, 128), 1)
    as_column = column(jnp.where(down == across, lens, 0.0))
    starts = jnp.sum(jnp.where(down < across, as_column, 0.0), axis=0, keepdims=True)
    rows = (first_row + lax.broadcasted_iota(jnp.int32, (ROWS, 128), 0)).astype(F32)
    own = jnp.max(jnp.where(starts <= rows, starts, 0.0), axis=1, keepdims=True)
    return own - first_row.astype(F32)


def kernel(
    tok_h, len_h, win_h, wout_h, gout_h,
    lo, gt, g_vk, g_q, g_uo,
    lens, win, wout, lo_v, gt_v,
    xg, gg, wc, xh, xn, xnt, xnp, xr, gate, qb, kv, slope, slope_p, srow,
    wt, sl, slt, wp,
    stat, gat, att, ee, dgate, datt, ds, dk, dv, dkv_s, dkv_r,
    din, din_s, din_r, stat2, dhid, dh_u, dh_q, dh_vk, pair,
    *rest,
):
    reduce_refs, (load_sem, out_sem, send_sem, recv_sem) = rest[:-4], rest[-4:]
    d, y = lax.axis_index("dp"), lax.axis_index("sub")
    c = lax.rem(d, NC)
    z = lax.rem(d // NC, NZ)
    x = d // (NC * NZ)
    ndp = NX * NZ * NC

    def at(ax, az, ac):
        return ((ax * NZ + az) * NC + ac, y)

    above = (lax.rem(d + 1, ndp), y)
    below = (lax.rem(d + ndp - 1, ndp), y)
    y_peers = [(r, lax.rem(y + r, NY)) for r in (2, 1, 3)]
    y_up, y_down = lax.rem(y + 1, NY), lax.rem(y + NY - 1, NY)

    loads = [
        pltpu.make_async_copy(src, dst, load_sem.at[i])
        for i, (src, dst) in enumerate(
            [
                (tok_h, xg.at[y]), (gout_h, gg.at[y]), (len_h, lens),
                (win_h, win), (wout_h, wout),
            ]
        )
    ]
    for load in loads:
        load.start()
    stores = []

    def put(src, dst):
        copy = pltpu.make_async_copy(src, dst, out_sem.at[len(stores)])
        copy.start()
        stores.append(copy)

    barrier = pltpu.get_barrier_semaphore()
    greet = [(d, peer) for _, peer in y_peers]
    greet += [at(lax.rem(x + r, NX), z, c) for r in range(1, NX)]
    greet += [at(x, lax.rem(z + r, NZ), c) for r in range(1, NZ)]
    greet += [at(x, z, 1 - c)]
    greet += [(lax.rem(d + ndp + 2 * c - 1, ndp), y)]
    for device in greet:
        pl.semaphore_signal(barrier, inc=1, device_id=device, device_id_type=MESH)
    for load in loads:
        load.wait()
    pl.semaphore_wait(barrier, len(greet))

    send = Sender(send_sem, recv_sem)
    core = (c, at(x, z, 1 - c))
    along_x = (NX, x, lambda to: at(to, z, c))
    along_z = (NZ, z, lambda to: at(x, to, c))
    scaling = 1.0 / math.sqrt(ROWS * ndp)
    r_uo = Reduce(send, core, along_x, along_z, reduce_refs[0:8], scaling)
    r_vk = Reduce3(send, core, along_z, along_x, reduce_refs[8:15], scaling)
    r_q = Reduce3(send, core, along_z, along_x, reduce_refs[15:22], scaling)
    tiles = [slice(t * TILE, (t + 1) * TILE) for t in range(ROWS // TILE)]
    half = ROWS // 2
    low, high = slice(0, half), slice(half, ROWS)

    def gather(own, whole):
        return send.group(whole, [(own, own, (d, peer)) for _, peer in y_peers])

    got_x = [gather(xg.at[y, rows], xg.at[0 : NY - 1, rows]) for rows in tiles[:-1]]
    pass_up = send(gg.at[y, low], gg.at[y, low], (d, y_up))
    pass_down = send(gg.at[y, high], gg.at[y, high], (d, y_down))
    rows = tiles[-1]
    got_x.append(gather(xg.at[y, rows], xg.at[0 : NY - 1, rows]))
    got_g = send.group(
        gg.at[0:2],
        [
            (gg.at[y, high], gg.at[y, high], (d, y_up)),
            (gg.at[y, low], gg.at[y, low], (d, y_down)),
        ],
    )
    srow[...] = jnp.broadcast_to(
        start_rows(lens, d * ROWS).astype(jnp.int32), (ROWS, 128)
    )
    wc[y] = wout[:, pl.ds(pl.multiple_of(y * HEAD, HEAD), HEAD)]
    root = 1.0 / math.sqrt(HEAD)

    def attend(scores, begin, first, causal):
        scores = scores * root
        col = lax.broadcasted_iota(jnp.int32, scores.shape, 1) + first
        allowed = col >= begin
        if causal is not None:
            row = lax.broadcasted_iota(jnp.int32, scores.shape, 0) + causal
            allowed = allowed & (col <= row)
        sig = 0.5 * jnp.tanh(0.5 * scores) + 0.5
        weight = jnp.where(allowed, scores * sig, 0.0).astype(BF)
        tangent = jnp.where(allowed, sig * (1.0 + scores * (1.0 - sig)) * root, 0.0)
        return weight, tangent

    got_kv = []
    for t, rows in enumerate(tiles):
        if t == len(tiles) - 1:
            pass_up.wait_recv()
            slot = gg.at[y_down, low]
            got_g.add(slot, slot, (d, y_up))
            pass_down.wait_recv()
            slot = gg.at[y_up, high]
            got_g.add(slot, slot, (d, y_down))
        got_x[t].wait_recv()
        parts = [xg[b, rows].astype(F32) for b in range(NY)]
        mean = column(parts[0] + parts[1] + parts[2] + parts[3]) * (1.0 / WIDTH)
        parts = [part - mean for part in parts]
        var = column(sum(part * part for part in parts)) * (1.0 / WIDTH)
        inv = lax.rsqrt(var + EPSILON)
        xr[rows, :] = jnp.broadcast_to(inv, (TILE, 128))
        for b in range(NY):
            hat = parts[b] * inv
            xh[b, rows] = hat
            xn[rows, b * HEAD : (b + 1) * HEAD] = hat.astype(BF)
        hidden = mm(xn[rows, :], win[...])
        sig = 0.5 * jnp.tanh(0.5 * hidden) + 0.5
        projected = (hidden * sig).astype(BF)
        own = slice(ROWS + t * TILE, ROWS + (t + 1) * TILE)
        kv[0, own] = projected[:, HEAD : 2 * HEAD]
        kv[1, own] = projected[:, 3 * HEAD :]
        got_kv.append(send(kv.at[:, own], kv.at[:, rows], above))
        gate[rows, :] = projected[:, :HEAD]
        qb[rows, :] = projected[:, 2 * HEAD : 3 * HEAD]
        slopes = sig * (1.0 + hidden * (1.0 - sig))
        for i, g in enumerate((0, 2, 1, 3)):
            slope[i, rows] = slopes[:, g * HEAD : (g + 1) * HEAD]

    for t, rows in enumerate(tiles):
        weight, tangent = attend(
            mm(qb[rows, :], kv[1, ROWS:], NT), srow[rows, 0:1], 0, t * TILE
        )
        wt[ROWS:, rows] = weight.T
        sl[rows, ROWS:] = tangent
        slt[ROWS:, rows] = tangent.T
        att[rows, :] = mm(weight, kv[0, ROWS:])
    got_xn = [send(xn.at[rows], xnp.at[rows], above) for rows in (low, high)]
    xnt[:, ROWS:] = xn[...].T

    for t, cols in enumerate(tiles):
        got_kv[t].wait_recv()
        weight, tangent = attend(
            mm(qb[...], kv[1, cols], NT), srow[...], t * TILE - ROWS, None
        )
        wp[:, cols] = weight
        sl[:, cols] = tangent
        att[...] = att[...] + mm(weight, kv[0, cols])

    got_g.wait_recv()
    d_gated = sum(
        mm(gg[b], wout[:, b * HEAD : (b + 1) * HEAD], NT) for b in range(NY)
    )
    dgate[...] = d_gated
    e = d_gated * gate[...].astype(F32)
    ee[...] = e

    a = att[...]
    sum_a = column(a)
    ca = a - sum_a * (1.0 / HEAD)
    lane = lax.broadcasted_iota(jnp.int32, (ROWS, 128), 1)
    packed = jnp.where(
        lane == 0, sum_a,
        jnp.where(lane == 1, column(ca * ca),
                  jnp.where(lane == 2, column(e), jnp.where(lane == 3, column(e * ca), 0.0))),
    )
    stat[y] = packed.T[:8]
    got_s = gather(stat.at[y], stat.at[0 : NY - 1])
    for rows in tiles:
        wt[rows, :] = wp[:, rows].T
        slt[rows, :] = sl[:, rows].T
    got_s.wait_recv()
    heads = [stat[h] for h in range(NY)]
    mean = sum(h[0:1] for h in heads) * (1.0 / WIDTH)
    var, s_e, s_en = 0.0, 0.0, 0.0
    for h in heads:
        off = h[0:1] * (1.0 / HEAD) - mean
        var = var + h[1:2] + HEAD * off * off
        s_e = s_e + h[2:3]
        s_en = s_en + h[3:4] + off * h[2:3]
    inv = lax.rsqrt(var * (1.0 / WIDTH) + EPSILON)
    line = lax.broadcasted_iota(jnp.int32, (128, ROWS), 0)
    back = jnp.where(
        line == 0, mean,
        jnp.where(line == 1, inv,
                  jnp.where(line == 2, s_e * (1.0 / WIDTH),
                            jnp.where(line == 3, s_en * inv * (1.0 / WIDTH), 0.0))),
    ).T
    mean, inv, s_e, s_en = [back[:, i : i + 1] for i in range(4)]
    normed = (att[...] - mean) * inv
    datt[...] = (inv * (ee[...] - s_e - normed * s_en)).astype(BF)
    gat[y] = (normed * gate[...].astype(F32)).astype(BF)
    got_a = gather(gat.at[y], gat.at[0 : NY - 1])
    got_w = send.group(
        wc.at[0 : NY - 1],
        [
            (
                wout.at[:, pl.ds(pl.multiple_of(peer * HEAD, HEAD), HEAD)],
                wc.at[y],
                (d, peer),
            )
            for _, peer in y_peers
        ],
    )
    dh_u[...] = (dgate[...] * normed * slope[0]).astype(BF)

    gated_t = gat[y].T
    pair[0] = mm(xnt[:, ROWS:], dh_u[...])
    for b in range(NY):
        pair[1, b * HEAD : (b + 1) * HEAD] = mm(gated_t, gg[b])
    r_uo.s1(pair[1 - c])
    r_uo.keep(pair[c])

    def key_grads(rows):
        d_st = (mm(kv[0, rows], datt[...], NT) * slt[rows, :]).astype(BF)
        dk[rows, :] = mm(d_st, qb[...])
        dv[rows, :] = mm(wt[rows, :], datt[...])

    for t in range(ROWS // TILE):
        key_grads(tiles[t])
    dkv_s[0] = dv[:ROWS, :].astype(BF)
    dkv_s[1] = dk[:ROWS, :].astype(BF)
    got_dkv = send(dkv_s, dkv_r, below)
    for t in range(ROWS // TILE):
        key_grads(slice(ROWS + t * TILE, ROWS + (t + 1) * TILE))
    r_uo.s2()

    for t, rows in enumerate((low, high)):
        got_xn[t].wait_recv()
        for i, g in enumerate((1, 3)):
            hidden = mm(xnp[rows, :], win[:, g * HEAD : (g + 1) * HEAD])
            sig = 0.5 * jnp.tanh(0.5 * hidden) + 0.5
            slope_p[i, rows] = sig * (1.0 + hidden * (1.0 - sig))
        xnt[:, rows] = xnp[rows, :].T
    dh_vk[:ROWS, :HEAD] = (dv[:ROWS, :] * slope_p[0]).astype(BF)
    dh_vk[:ROWS, HEAD:] = (dk[:ROWS, :] * slope_p[1]).astype(BF)
    dh_vk[ROWS:, :HEAD] = (dv[ROWS:, :] * slope[2]).astype(BF)
    dh_vk[ROWS:, HEAD:] = (dk[ROWS:, :] * slope[3]).astype(BF)
    mine = pl.ds(pl.multiple_of(c * half, half), half)
    theirs = pl.ds(pl.multiple_of((1 - c) * half, half), half)
    r_vk.s1(mm(xnt[theirs, :], dh_vk[...]))

    for rows in tiles:
        ds[rows, :] = (mm(datt[rows, :], kv[0], NT) * sl[rows, :]).astype(BF)
        dq = mm(ds[rows, :], kv[1])
        dh_q[rows, :] = (dq * slope[1, rows]).astype(BF)
    r_q.s1(mm(xnt[theirs, ROWS:], dh_q[...]))
    r_vk.keep(mm(xnt[mine, :], dh_vk[...]))
    r_vk.s2()
    r_q.keep(mm(xnt[mine, ROWS:], dh_q[...]))
    r_q.s2()
    r_uo.s3()

    dhid[:, 0:HEAD] = dh_u[...]
    dhid[:, 2 * HEAD : 3 * HEAD] = dh_q[...]
    got_dkv.wait_recv()
    dhid[:, HEAD : 2 * HEAD] = ((dv[ROWS:, :] + dkv_r[0].astype(F32)) * slope[2]).astype(BF)
    dhid[:, 3 * HEAD :] = ((dk[ROWS:, :] + dkv_r[1].astype(F32)) * slope[3]).astype(BF)
    one, two = 0.0, 0.0
    for b in range(NY):
        part = mm(dhid[...], win[b * HEAD : (b + 1) * HEAD, :], NT)
        one = one + part
        two = two + part * xh[b]
        din[b] = part
        din_s[b] = part.astype(BF)
    packed = jnp.where(lane == 0, column(one), jnp.where(lane == 1, column(two), 0.0))
    stat2[y] = packed.T[:8]
    got_i = send.group(
        din_r, [(din_s.at[peer], din_r.at[r - 1], (d, peer)) for r, peer in y_peers]
    )
    got_t = gather(stat2.at[y], stat2.at[0 : NY - 1])

    got_a.wait_recv()
    got_w.wait_recv()
    lo_v[...] = (
        xg[y].astype(F32) + sum(mm(gat[h], wc[h]) for h in range(NY))
    ).astype(BF)
    put(lo_v, lo)
    r_vk.s3()
    r_q.s3()
    r_uo.s4()
    r_vk.s4()
    r_q.s4()
    r_uo.s5()

    got_i.wait_recv()
    got_t.wait_recv()
    total = din[y]
    for r in range(NY - 1):
        total = total + din_r[r].astype(F32)
    both = (stat2[0] + stat2[1] + stat2[2] + stat2[3]) * (1.0 / WIDTH)
    back = jnp.where(line == 0, both[0:1], jnp.where(line == 1, both[1:2], 0.0)).T
    piece = xr[:, 0:1] * (total - back[:, 0:1] - xh[y] * back[:, 1:2])
    gt_v[...] = (gg[y].astype(F32) + piece).astype(BF)
    put(gt_v, gt)

    r_vk.s5()
    r_q.s5()
    r_uo.s6()
    r_vk.s6()
    put(r_vk.full, g_vk)
    r_q.s6()
    put(r_q.full, g_q)
    r_uo.s7()
    put(r_uo.full, g_uo)
    for w in send.groups:
        w.wait_send()
    for w in stores:
        w.wait()


def store(
    lo_h, gt_h, vk_h, q_h, uo_h, lo, gt, gwin, gwout,
    lo_v, gt_v, vk, q, uo, gwin_v, gwout_v, read_sem, write_sem,
):
    pairs = [(lo_h, lo_v), (gt_h, gt_v), (vk_h, vk), (q_h, q), (uo_h, uo)]
    reads = [
        pltpu.make_async_copy(src, dst, read_sem.at[i]) for i, (src, dst) in enumerate(pairs)
    ]
    writes = []

    def write(src, dst):
        writes.append(pltpu.make_async_copy(src, dst, write_sem.at[len(writes)]))
        writes[-1].start()

    def write_columns(g, value):
        cols = slice(g * HEAD, (g + 1) * HEAD)
        gwin_v[:, cols] = value.reshape(ROWS, HEAD).astype(F32)
        write(gwin_v.at[:, cols], gwin.at[:, cols])

    for i in (2, 3, 4, 0, 1):
        reads[i].start()
    reads[2].wait()
    write_columns(1, vk[:, :, :, :HEAD])
    write_columns(3, vk[:, :, :, HEAD:])
    reads[3].wait()
    write_columns(2, q[...])
    reads[4].wait()
    write_columns(0, uo[0])
    for b in range(NY):
        gwout_v[:, b * HEAD : (b + 1) * HEAD] = uo[1, b].reshape(HEAD, HEAD).astype(F32)
    write(gwout_v, gwout)
    reads[0].wait()
    write(lo_v, lo)
    reads[1].wait()
    write(gt_v, gt)
    for copy in writes:
        copy.wait()


def reduce3_scratch(n):
    r = ROWS // (NC * NZ)
    block = (NZ, r, n)
    return [
        pltpu.VMEM(block, F32),
        pltpu.VMEM(block, BF),
        pltpu.VMEM(block, BF),
        pltpu.VMEM(block, BF),
        pltpu.VMEM((NZ - 1, r, n), BF),
        pltpu.VMEM((NX, r, n), BF),
        pltpu.VMEM((NC,) + block, BF),
    ]


def reduce_scratch(n1, n2, rows, dt):
    block = (n1, n2, rows, HEAD)
    return [
        pltpu.VMEM(block, F32),
        pltpu.VMEM(block, dt),
        pltpu.VMEM(block, dt),
        pltpu.VMEM(block, dt),
        pltpu.VMEM((n1 - 1, n2, rows, HEAD), dt),
        pltpu.VMEM((n2, rows, HEAD), dt),
        pltpu.VMEM((n2 - 1, rows, HEAD), dt),
        pltpu.VMEM((NC,) + block, dt),
    ]


def shards(tokens, lengths, weight_in, weight_out, grad_out):
    lengths = lengths.reshape(1, -1)
    hbm = pl.BlockSpec(memory_space=pltpu.HBM)
    blocks = lambda n, dt: pltpu.VMEM((n, ROWS, HEAD), dt)
    full = lambda dt: pltpu.VMEM((ROWS, WIDTH), dt)
    one = lambda dt: pltpu.VMEM((ROWS, HEAD), dt)
    tall = lambda n, dt: pltpu.VMEM((2 * ROWS, n), dt)
    stats = pltpu.VMEM((NY, 8, ROWS), F32)
    scratch = [
        pltpu.VMEM((1, 128), jnp.int32), full(BF), pltpu.VMEM((HEAD, WIDTH), BF),
        one(BF), one(BF),
        blocks(NY, BF), blocks(NY, BF), pltpu.VMEM((NY, HEAD, HEAD), BF),
        blocks(NY, F32), full(BF), pltpu.VMEM((WIDTH, 2 * ROWS), BF), full(BF), one(F32),
        one(BF), one(BF), pltpu.VMEM((2, 2 * ROWS, HEAD), BF), blocks(4, F32),
        blocks(2, F32), one(jnp.int32),
        tall(ROWS, BF), pltpu.VMEM((ROWS, 2 * ROWS), F32), tall(ROWS, F32), full(BF),
        stats, blocks(NY, BF), one(F32), one(F32), one(F32), one(BF),
        pltpu.VMEM((ROWS, 2 * ROWS), BF), tall(HEAD, F32), tall(HEAD, F32),
        blocks(2, BF), blocks(2, BF),
        blocks(NY, F32), blocks(NY, BF), blocks(NY - 1, BF), stats,
        full(BF), one(BF), one(BF), tall(2 * HEAD, BF), blocks(2, F32),
        *reduce_scratch(NX, NZ, 16, BF),
        *reduce3_scratch(2 * HEAD),
        *reduce3_scratch(HEAD),
        pltpu.SemaphoreType.DMA((5,)),
        pltpu.SemaphoreType.DMA((5,)),
        pltpu.SemaphoreType.DMA((39,)),
        pltpu.SemaphoreType.DMA((39,)),
    ]
    rounded = (
        (ROWS, HEAD),
        (ROWS, HEAD),
        (NC, NZ, ROWS // (NC * NZ), 2 * HEAD),
        (NC, NZ, ROWS // (NC * NZ), HEAD),
        (NC, NX, NZ, 16, HEAD),
    )
    shapes = (
        jax.ShapeDtypeStruct((ROWS, HEAD), BF),
        jax.ShapeDtypeStruct((ROWS, HEAD), BF),
        jax.ShapeDtypeStruct((WIDTH, 4 * HEAD), F32),
        jax.ShapeDtypeStruct((HEAD, WIDTH), F32),
    )
    results = pl.pallas_call(
        kernel,
        out_shape=tuple(jax.ShapeDtypeStruct(shape, BF) for shape in rounded),
        in_specs=[hbm] * 5,
        out_specs=(hbm,) * 5,
        scratch_shapes=scratch,
        compiler_params=pltpu.CompilerParams(
            collective_id=0, has_side_effects=True, vmem_limit_bytes=62 * 1024 * 1024
        ),
        name="layer",
    )(tokens, lengths, weight_in, weight_out, grad_out)
    return pl.pallas_call(
        store,
        out_shape=shapes,
        in_specs=[hbm] * 5,
        out_specs=(hbm,) * 4,
        scratch_shapes=[pltpu.VMEM(shape, BF) for shape in rounded]
        + [full(F32), pltpu.VMEM((HEAD, WIDTH), F32)]
        + [pltpu.SemaphoreType.DMA((5,)), pltpu.SemaphoreType.DMA((7,))],
        compiler_params=pltpu.CompilerParams(vmem_limit_bytes=62 * 1024 * 1024),
        name="store",
    )(*results)


def solution(mesh):
    placed = (P("dp", "sub"), P(), P(None, "sub"), P("sub", None), P("dp", "sub"))
    return jax.shard_map(
        shards,
        mesh=mesh,
        in_specs=placed,
        out_specs=(P("dp", "sub"), P("dp", "sub"), P(None, "sub"), P("sub", None)),
        check_vma=False,
    )
```

```python
import functools
import math

import jax
import jax.numpy as jnp
from jax import lax
from jax.experimental import pallas as pl
from jax.experimental.pallas import tpu as pltpu
from jax.sharding import PartitionSpec as P

EPSILON = 1e-05
NX, NZ, NC, NY = 4, 8, 2, 4
ROWS, HEAD, WIDTH = 512, 128, 512
TILE = 128
MESH = pl.DeviceIdType.MESH
BF, F32 = jnp.bfloat16, jnp.float32

NN = (((1,), (0,)), ((), ()))
NT = (((1,), (1,)), ((), ()))
TN = (((0,), (0,)), ((), ()))


def mm(left, right, dims=NN):
    return lax.dot_general(left, right, dims, preferred_element_type=F32)


class Exchange:
    def __init__(self, make, whole):
        self.make, self.whole = make, whole

    def add(self, src, dst, device):
        self.make(src, dst, device).start()
        self.device = device
        return self

    def wait_recv(self):
        self.make(self.whole, self.whole, self.device).wait_recv()

    def wait_send(self):
        self.make(self.whole, self.whole, self.device).wait_send()


class Sender:
    def __init__(self, send_sem, recv_sem):
        self.send_sem, self.recv_sem, self.groups = send_sem, recv_sem, []

    def group(self, whole, copies=()):
        i = len(self.groups)

        def make(src, dst, device):
            return pltpu.make_async_remote_copy(
                src_ref=src,
                dst_ref=dst,
                send_sem=self.send_sem.at[i],
                recv_sem=self.recv_sem.at[i],
                device_id=device,
                device_id_type=MESH,
            )

        group = Exchange(make, whole)
        self.groups.append(group)
        for src, dst, device in copies:
            group.add(src, dst, device)
        return group

    def __call__(self, src, dst, device):
        return self.group(src, [(src, dst, device)])


def far_first(n):
    return sorted(range(1, n), key=lambda r: (-min(r, n - r), r))


class Reduce:
    def __init__(self, send, core, first, second, refs, scale):
        self.send, self.scale = send, scale
        self.c, self.core = core
        self.n1, self.i1, self.at1 = first
        self.n2, self.i2, self.at2 = second
        self.part, self.sb, self.rc, self.s_1, self.r_1, self.s_2, self.r_2, self.full = refs
        self.dt = self.full.dtype

    def to1(self, r):
        return lax.rem(self.i1 + r, self.n1)

    def to2(self, r):
        return lax.rem(self.i2 + r, self.n2)

    def s1(self, other):
        self.sb[...] = other.astype(self.dt).reshape(self.sb.shape)
        self.w1 = self.send(self.sb, self.rc, self.core)

    def keep(self, own):
        self.part[...] = own.reshape(self.part.shape)

    def s2(self):
        self.w1.wait_recv()
        total = self.part[...] + self.rc[...].astype(F32)
        self.part[...] = total
        self.s_1[...] = total.astype(self.dt)
        self.w2 = self.send.group(self.r_1)
        for r in far_first(self.n1):
            to = self.to1(r)
            self.w2.add(self.s_1.at[to], self.r_1.at[r - 1], self.at1(to))

    def s3(self):
        self.w2.wait_recv()
        total = self.part[self.i1]
        for r in range(self.n1 - 1):
            total = total + self.r_1[r].astype(F32)
        self.part[0] = total
        self.s_2[...] = total.astype(self.dt)
        self.w3 = self.send.group(self.r_2)
        for r in far_first(self.n2):
            to = self.to2(r)
            self.w3.add(self.s_2.at[to], self.r_2.at[r - 1], self.at2(to))

    def s4(self):
        self.w3.wait_recv()
        total = self.part[0, self.i2]
        for r in range(self.n2 - 1):
            total = total + self.r_2[r].astype(F32)
        mine = self.full.at[self.c, self.i1, self.i2]
        self.full[self.c, self.i1, self.i2] = (total * self.scale).astype(self.dt)
        self.w4 = self.send.group(
            self.r_2, [(mine, mine, self.at2(self.to2(r))) for r in far_first(self.n2)]
        )

    def s5(self):
        self.w4.wait_recv()
        mine = self.full.at[self.c, self.i1]
        self.w5 = [
            (r, self.send(mine, mine, self.at1(self.to1(r)))) for r in far_first(self.n1)
        ]
        self.w6 = self.send.group(self.s_1, [(mine, mine, self.core)])

    def s6(self):
        for r, w in self.w5[::-1]:
            w.wait_recv()
            piece = self.full.at[self.c, lax.rem(self.i1 + self.n1 - r, self.n1)]
            self.w6.add(piece, piece, self.core)

    def s7(self):
        self.w6.wait_recv()


class Reduce3:
    def __init__(self, send, core, first, second, refs, scale):
        self.send, self.scale = send, scale
        self.c, self.core = core
        self.n1, self.i1, self.at1 = first
        self.n2, self.i2, self.at2 = second
        self.part, self.sb, self.rc, self.s_1, self.r_1, self.both, self.full = refs
        self.dt = self.full.dtype

    def s1(self, other):
        self.sb[...] = other.astype(self.dt).reshape(self.sb.shape)
        self.w1 = self.send(self.sb, self.rc, self.core)

    def keep(self, own):
        self.part[...] = own.reshape(self.part.shape)

    def s2(self):
        self.w1.wait_recv()
        total = self.part[...] + self.rc[...].astype(F32)
        self.part[...] = total
        self.s_1[...] = total.astype(self.dt)
        self.w2 = self.send.group(self.r_1)
        for r in far_first(self.n1):
            to = lax.rem(self.i1 + r, self.n1)
            self.w2.add(self.s_1.at[to], self.r_1.at[r - 1], self.at1(to))

    def s3(self):
        self.w2.wait_recv()
        total = self.part[self.i1]
        for r in range(self.n1 - 1):
            total = total + self.r_1[r].astype(F32)
        self.both[self.i2] = total.astype(self.dt)
        mine = self.both.at[self.i2]
        self.w3 = self.send.group(
            self.both.at[0 : self.n2 - 1],
            [
                (mine, mine, self.at2(lax.rem(self.i2 + r, self.n2)))
                for r in far_first(self.n2)
            ],
        )

    def s4(self):
        self.w3.wait_recv()
        total = self.both[0].astype(F32)
        for k in range(1, self.n2):
            total = total + self.both[k].astype(F32)
        self.full[self.c, self.i1] = (total * self.scale).astype(self.dt)
        mine = self.full.at[self.c, self.i1]
        order = far_first(self.n1)
        self.w4 = []
        for steps in (order[:3], order[3:]):
            peers = [self.at1(lax.rem(self.i1 + r, self.n1)) for r in steps]
            whole = self.r_1.at[0 : len(steps)]
            self.w4.append((steps, self.send.group(whole, [(mine, mine, to) for to in peers])))
        self.w5 = self.send.group(self.s_1, [(mine, mine, self.core)])

    def s5(self):
        for steps, w in self.w4[::-1]:
            w.wait_recv()
            for r in steps:
                piece = self.full.at[self.c, lax.rem(self.i1 + self.n1 - r, self.n1)]
                self.w5.add(piece, piece, self.core)

    def s6(self):
        self.w5.wait_recv()


def column(value):
    return jnp.sum(value, axis=1, keepdims=True)


def start_rows(lens_ref, first_row):
    lens = jnp.broadcast_to(lens_ref[...].astype(F32), (128, 128))
    down = lax.broadcasted_iota(jnp.int32, (128, 128), 0)
    across = lax.broadcasted_iota(jnp.int32, (128, 128), 1)
    as_column = column(jnp.where(down == across, lens, 0.0))
    starts = jnp.sum(jnp.where(down < across, as_column, 0.0), axis=0, keepdims=True)
    rows = (first_row + lax.broadcasted_iota(jnp.int32, (ROWS, 128), 0)).astype(F32)
    own = jnp.max(jnp.where(starts <= rows, starts, 0.0), axis=1, keepdims=True)
    return own - first_row.astype(F32)


def kernel(
    tok_h, len_h, win_h, wout_h, gout_h,
    lo, gt, g_vk, g_q, g_uo,
    lens, win, wout, lo_v, gt_v,
    xg, gg, wc, xh, xn, xnt, xnp, xr, gate, qb, kv, slope, slope_p, srow,
    wt, sl, slt, wp,
    stat, gat, att, ee, dgate, datt, ds, dk, dv, dkv_s, dkv_r,
    din, din_s, din_r, stat2, dhid, dh_u, dh_q, dh_vk, left, right,
    *rest,
):
    reduce_refs, (load_sem, out_sem, send_sem, recv_sem) = rest[:-4], rest[-4:]
    d, y = lax.axis_index("dp"), lax.axis_index("sub")
    c = lax.rem(d, NC)
    z = lax.rem(d // NC, NZ)
    x = d // (NC * NZ)
    ndp = NX * NZ * NC

    def at(ax, az, ac):
        return ((ax * NZ + az) * NC + ac, y)

    above = (lax.rem(d + 1, ndp), y)
    below = (lax.rem(d + ndp - 1, ndp), y)
    y_peers = [(r, lax.rem(y + r, NY)) for r in (2, 1, 3)]
    y_up, y_down = lax.rem(y + 1, NY), lax.rem(y + NY - 1, NY)

    loads = [
        pltpu.make_async_copy(src, dst, load_sem.at[i])
        for i, (src, dst) in enumerate(
            [
                (tok_h, xg.at[y]), (gout_h, gg.at[y]), (len_h, lens),
                (win_h, win), (wout_h, wout),
            ]
        )
    ]
    for load in loads:
        load.start()
    stores = []

    def put(src, dst):
        copy = pltpu.make_async_copy(src, dst, out_sem.at[len(stores)])
        copy.start()
        stores.append(copy)

    barrier = pltpu.get_barrier_semaphore()
    greet = [at(x, lax.rem(z + r, NZ), c) for r in far_first(NZ)]
    greet += [at(lax.rem(x + r, NX), z, c) for r in far_first(NX)]
    greet += [(d, peer) for _, peer in y_peers]
    greet += [(lax.rem(d + ndp + 2 * c - 1, ndp), y)]
    greet += [at(x, z, 1 - c)]
    for device in greet:
        pl.semaphore_signal(barrier, inc=1, device_id=device, device_id_type=MESH)
    for load in loads:
        load.wait()
    pl.semaphore_wait(barrier, len(greet))

    send = Sender(send_sem, recv_sem)
    core = (c, at(x, z, 1 - c))
    along_x = (NX, x, lambda to: at(to, z, c))
    along_z = (NZ, z, lambda to: at(x, to, c))
    scaling = 1.0 / math.sqrt(ROWS * ndp)
    r_uo = Reduce(send, core, along_x, along_z, reduce_refs[0:8], scaling)
    r_vk = Reduce3(send, core, along_z, along_x, reduce_refs[8:15], scaling)
    r_q = Reduce3(send, core, along_z, along_x, reduce_refs[15:22], scaling)
    tiles = [slice(t * TILE, (t + 1) * TILE) for t in range(ROWS // TILE)]
    half = ROWS // 2
    low, high = slice(0, half), slice(half, ROWS)

    def gather(own, whole):
        return send.group(whole, [(own, own, (d, peer)) for _, peer in y_peers])

    got_x = [gather(xg.at[y, rows], xg.at[0 : NY - 1, rows]) for rows in tiles[:-1]]
    pass_up = send(gg.at[y, low], gg.at[y, low], (d, y_up))
    pass_down = send(gg.at[y, high], gg.at[y, high], (d, y_down))
    rows = tiles[-1]
    got_x.append(gather(xg.at[y, rows], xg.at[0 : NY - 1, rows]))
    got_g = send.group(
        gg.at[0:2],
        [
            (gg.at[y, high], gg.at[y, high], (d, y_up)),
            (gg.at[y, low], gg.at[y, low], (d, y_down)),
        ],
    )
    srow[...] = jnp.broadcast_to(
        start_rows(lens, d * ROWS).astype(jnp.int32), (ROWS, 128)
    )
    wc[y] = wout[:, pl.ds(pl.multiple_of(y * HEAD, HEAD), HEAD)]
    root = 1.0 / math.sqrt(HEAD)

    def attend(scores, begin, first, causal):
        scores = scores * root
        col = lax.broadcasted_iota(jnp.int32, scores.shape, 1) + first
        allowed = col >= begin
        if causal is not None:
            row = lax.broadcasted_iota(jnp.int32, scores.shape, 0) + causal
            allowed = allowed & (col <= row)
        sig = 0.5 * jnp.tanh(0.5 * scores) + 0.5
        weight = jnp.where(allowed, scores * sig, 0.0).astype(BF)
        tangent = jnp.where(allowed, sig * (1.0 + scores * (1.0 - sig)) * root, 0.0)
        return weight, tangent

    got_kv = []
    for t, rows in enumerate(tiles):
        if t == len(tiles) - 1:
            pass_up.wait_recv()
            slot = gg.at[y_down, low]
            got_g.add(slot, slot, (d, y_up))
            pass_down.wait_recv()
            slot = gg.at[y_up, high]
            got_g.add(slot, slot, (d, y_down))
        got_x[t].wait_recv()
        parts = [xg[b, rows].astype(F32) for b in range(NY)]
        mean = column(parts[0] + parts[1] + parts[2] + parts[3]) * (1.0 / WIDTH)
        parts = [part - mean for part in parts]
        var = column(sum(part * part for part in parts)) * (1.0 / WIDTH)
        inv = lax.rsqrt(var + EPSILON)
        xr[rows, :] = jnp.broadcast_to(inv, (TILE, 128))
        for b in range(NY):
            hat = parts[b] * inv
            xh[b, rows] = hat
            xn[rows, b * HEAD : (b + 1) * HEAD] = hat.astype(BF)
        hidden = mm(xn[rows, :], win[...])
        sig = 0.5 * jnp.tanh(0.5 * hidden) + 0.5
        projected = (hidden * sig).astype(BF)
        own = slice(ROWS + t * TILE, ROWS + (t + 1) * TILE)
        kv[0, own] = projected[:, HEAD : 2 * HEAD]
        kv[1, own] = projected[:, 3 * HEAD :]
        got_kv.append(send(kv.at[:, own], kv.at[:, rows], above))
        gate[rows, :] = projected[:, :HEAD]
        qb[rows, :] = projected[:, 2 * HEAD : 3 * HEAD]
        slopes = sig * (1.0 + hidden * (1.0 - sig))
        for i, g in enumerate((0, 2, 1, 3)):
            slope[i, rows] = slopes[:, g * HEAD : (g + 1) * HEAD]

    for t, rows in enumerate(tiles):
        weight, tangent = attend(
            mm(qb[rows, :], kv[1, ROWS:], NT), srow[rows, 0:1], 0, t * TILE
        )
        wt[ROWS:, rows] = weight.T
        sl[rows, ROWS:] = tangent
        slt[ROWS:, rows] = tangent.T
        att[rows, :] = mm(weight, kv[0, ROWS:])
    got_xn = [send(xn.at[rows], xnp.at[rows], above) for rows in (low, high)]
    xnt[:, ROWS:] = xn[...].T

    for t, cols in enumerate(tiles):
        got_kv[t].wait_recv()
        weight, tangent = attend(
            mm(qb[...], kv[1, cols], NT), srow[...], t * TILE - ROWS, None
        )
        wp[:, cols] = weight
        sl[:, cols] = tangent
        att[...] = att[...] + mm(weight, kv[0, cols])

    got_g.wait_recv()
    d_gated = sum(
        mm(gg[b], wout[:, b * HEAD : (b + 1) * HEAD], NT) for b in range(NY)
    )
    dgate[...] = d_gated
    e = d_gated * gate[...].astype(F32)
    ee[...] = e

    a = att[...]
    sum_a = column(a)
    ca = a - sum_a * (1.0 / HEAD)
    lane = lax.broadcasted_iota(jnp.int32, (ROWS, 128), 1)
    packed = jnp.where(
        lane == 0, sum_a,
        jnp.where(lane == 1, column(ca * ca),
                  jnp.where(lane == 2, column(e), jnp.where(lane == 3, column(e * ca), 0.0))),
    )
    stat[y] = packed.T[:8]
    got_s = gather(stat.at[y], stat.at[0 : NY - 1])
    for rows in tiles:
        wt[rows, :] = wp[:, rows].T
        slt[rows, :] = sl[:, rows].T
    def block_before(t, rows):
        got_xn[t].wait_recv()
        for i, g in enumerate((1, 3)):
            hidden = mm(xnp[rows, :], win[:, g * HEAD : (g + 1) * HEAD])
            sig = 0.5 * jnp.tanh(0.5 * hidden) + 0.5
            slope_p[i, rows] = sig * (1.0 + hidden * (1.0 - sig))
        xnt[:, rows] = xnp[rows, :].T

    for b in range(NY):
        left[1, b * HEAD : (b + 1) * HEAD] = gg[b].T
    left[0] = xnt[:, ROWS:]
    block_before(0, low)
    got_s.wait_recv()
    heads = [stat[h] for h in range(NY)]
    mean = sum(h[0:1] for h in heads) * (1.0 / WIDTH)
    var, s_e, s_en = 0.0, 0.0, 0.0
    for h in heads:
        off = h[0:1] * (1.0 / HEAD) - mean
        var = var + h[1:2] + HEAD * off * off
        s_e = s_e + h[2:3]
        s_en = s_en + h[3:4] + off * h[2:3]
    inv = lax.rsqrt(var * (1.0 / WIDTH) + EPSILON)
    line = lax.broadcasted_iota(jnp.int32, (128, ROWS), 0)
    back = jnp.where(
        line == 0, mean,
        jnp.where(line == 1, inv,
                  jnp.where(line == 2, s_e * (1.0 / WIDTH),
                            jnp.where(line == 3, s_en * inv * (1.0 / WIDTH), 0.0))),
    ).T
    mean, inv, s_e, s_en = [back[:, i : i + 1] for i in range(4)]
    normed = (att[...] - mean) * inv
    datt[...] = (inv * (ee[...] - s_e - normed * s_en)).astype(BF)
    gat[y] = (normed * gate[...].astype(F32)).astype(BF)
    got_a = gather(gat.at[y], gat.at[0 : NY - 1])
    got_w = send.group(
        wc.at[0 : NY - 1],
        [
            (
                wout.at[:, pl.ds(pl.multiple_of(peer * HEAD, HEAD), HEAD)],
                wc.at[y],
                (d, peer),
            )
            for _, peer in y_peers
        ],
    )
    dh_u[...] = (dgate[...] * normed * slope[0]).astype(BF)

    right[0] = dh_u[...]
    right[1] = gat[y]
    r_uo.s1(mm(left[1 - c], right[1 - c]))

    def key_grads(rows, first):
        d_st = (mm(kv[0, rows], datt[first:, :], NT) * slt[rows, first:]).astype(BF)
        dk[rows, :] = mm(d_st, qb[first:, :])
        dv[rows, :] = mm(wt[rows, first:], datt[first:, :])

    for t in range(ROWS // TILE):
        key_grads(tiles[t], 0)
    dkv_s[0] = dv[:ROWS, :].astype(BF)
    dkv_s[1] = dk[:ROWS, :].astype(BF)
    got_dkv = send(dkv_s, dkv_r, below)
    r_uo.keep(mm(left[c], right[c]))
    r_uo.s2()
    for t in range(ROWS // TILE):
        key_grads(slice(ROWS + t * TILE, ROWS + (t + 1) * TILE), t * TILE)

    block_before(1, high)
    dh_vk[:ROWS, :HEAD] = (dv[:ROWS, :] * slope_p[0]).astype(BF)
    dh_vk[:ROWS, HEAD:] = (dk[:ROWS, :] * slope_p[1]).astype(BF)
    dh_vk[ROWS:, :HEAD] = (dv[ROWS:, :] * slope[2]).astype(BF)
    dh_vk[ROWS:, HEAD:] = (dk[ROWS:, :] * slope[3]).astype(BF)
    mine = pl.ds(pl.multiple_of(c * half, half), half)
    theirs = pl.ds(pl.multiple_of((1 - c) * half, half), half)
    r_vk.s1(mm(xnt[theirs, :], dh_vk[...]))

    for rows in tiles:
        ds[rows, :] = (mm(datt[rows, :], kv[0], NT) * sl[rows, :]).astype(BF)
        dq = mm(ds[rows, :], kv[1])
        dh_q[rows, :] = (dq * slope[1, rows]).astype(BF)
    r_q.s1(mm(xnt[theirs, ROWS:], dh_q[...]))
    r_vk.keep(mm(xnt[mine, :], dh_vk[...]))
    r_vk.s2()
    r_q.keep(mm(xnt[mine, ROWS:], dh_q[...]))
    r_q.s2()
    r_uo.s3()

    dhid[:, 0:HEAD] = dh_u[...]
    dhid[:, 2 * HEAD : 3 * HEAD] = dh_q[...]
    got_dkv.wait_recv()
    dhid[:, HEAD : 2 * HEAD] = ((dv[ROWS:, :] + dkv_r[0].astype(F32)) * slope[2]).astype(BF)
    dhid[:, 3 * HEAD :] = ((dk[ROWS:, :] + dkv_r[1].astype(F32)) * slope[3]).astype(BF)
    one, two = 0.0, 0.0
    for b in range(NY):
        part = mm(dhid[...], win[b * HEAD : (b + 1) * HEAD, :], NT)
        one = one + part
        two = two + part * xh[b]
        din[b] = part
        din_s[b] = part.astype(BF)
    packed = jnp.where(lane == 0, column(one), jnp.where(lane == 1, column(two), 0.0))
    stat2[y] = packed.T[:8]
    got_i = send.group(
        din_r, [(din_s.at[peer], din_r.at[r - 1], (d, peer)) for r, peer in y_peers]
    )
    got_t = gather(stat2.at[y], stat2.at[0 : NY - 1])

    got_a.wait_recv()
    got_w.wait_recv()
    lo_v[...] = (
        xg[y].astype(F32) + sum(mm(gat[h], wc[h]) for h in range(NY))
    ).astype(BF)
    put(lo_v, lo)
    r_vk.s3()
    r_uo.s4()
    r_q.s3()
    r_vk.s4()
    r_q.s4()
    r_uo.s5()

    got_i.wait_recv()
    got_t.wait_recv()
    total = din[y]
    for r in range(NY - 1):
        total = total + din_r[r].astype(F32)
    both = (stat2[0] + stat2[1] + stat2[2] + stat2[3]) * (1.0 / WIDTH)
    back = jnp.where(line == 0, both[0:1], jnp.where(line == 1, both[1:2], 0.0)).T
    piece = xr[:, 0:1] * (total - back[:, 0:1] - xh[y] * back[:, 1:2])
    gt_v[...] = (gg[y].astype(F32) + piece).astype(BF)
    put(gt_v, gt)

    r_vk.s5()
    r_q.s5()
    r_uo.s6()
    r_vk.s6()
    put(r_vk.full, g_vk)
    r_q.s6()
    put(r_q.full, g_q)
    r_uo.s7()
    put(r_uo.full, g_uo)
    for w in send.groups:
        w.wait_send()
    for w in stores:
        w.wait()


def store(
    lo_h, gt_h, vk_h, q_h, uo_h, lo, gt, gwin, gwout,
    lo_v, gt_v, vk, q, uo, gwin_v, gwout_v, read_sem, write_sem,
):
    pairs = [(lo_h, lo_v), (gt_h, gt_v), (vk_h, vk), (q_h, q), (uo_h, uo)]
    reads = [
        pltpu.make_async_copy(src, dst, read_sem.at[i]) for i, (src, dst) in enumerate(pairs)
    ]
    writes = []

    def write(src, dst):
        writes.append(pltpu.make_async_copy(src, dst, write_sem.at[len(writes)]))
        writes[-1].start()

    def write_columns(g, value):
        cols = slice(g * HEAD, (g + 1) * HEAD)
        gwin_v[:, cols] = value.reshape(ROWS, HEAD).astype(F32)
        write(gwin_v.at[:, cols], gwin.at[:, cols])

    for i in (2, 3, 4, 0, 1):
        reads[i].start()
    reads[2].wait()
    write_columns(1, vk[:, :, :, :HEAD])
    write_columns(3, vk[:, :, :, HEAD:])
    reads[3].wait()
    write_columns(2, q[...])
    reads[4].wait()
    write_columns(0, uo[0])
    gwout_v[...] = uo[1].reshape(WIDTH, HEAD).astype(F32).T
    write(gwout_v, gwout)
    reads[0].wait()
    write(lo_v, lo)
    reads[1].wait()
    write(gt_v, gt)
    for copy in writes:
        copy.wait()


def reduce3_scratch(n):
    r = ROWS // (NC * NZ)
    block = (NZ, r, n)
    return [
        pltpu.VMEM(block, F32),
        pltpu.VMEM(block, BF),
        pltpu.VMEM(block, BF),
        pltpu.VMEM(block, BF),
        pltpu.VMEM((NZ - 1, r, n), BF),
        pltpu.VMEM((NX, r, n), BF),
        pltpu.VMEM((NC,) + block, BF),
    ]


def reduce_scratch(n1, n2, rows, dt):
    block = (n1, n2, rows, HEAD)
    return [
        pltpu.VMEM(block, F32),
        pltpu.VMEM(block, dt),
        pltpu.VMEM(block, dt),
        pltpu.VMEM(block, dt),
        pltpu.VMEM((n1 - 1, n2, rows, HEAD), dt),
        pltpu.VMEM((n2, rows, HEAD), dt),
        pltpu.VMEM((n2 - 1, rows, HEAD), dt),
        pltpu.VMEM((NC,) + block, dt),
    ]


def shards(tokens, lengths, weight_in, weight_out, grad_out):
    lengths = lengths.reshape(1, -1)
    hbm = pl.BlockSpec(memory_space=pltpu.HBM)
    blocks = lambda n, dt: pltpu.VMEM((n, ROWS, HEAD), dt)
    full = lambda dt: pltpu.VMEM((ROWS, WIDTH), dt)
    one = lambda dt: pltpu.VMEM((ROWS, HEAD), dt)
    tall = lambda n, dt: pltpu.VMEM((2 * ROWS, n), dt)
    stats = pltpu.VMEM((NY, 8, ROWS), F32)
    scratch = [
        pltpu.VMEM((1, 128), jnp.int32), full(BF), pltpu.VMEM((HEAD, WIDTH), BF),
        one(BF), one(BF),
        blocks(NY, BF), blocks(NY, BF), pltpu.VMEM((NY, HEAD, HEAD), BF),
        blocks(NY, F32), full(BF), pltpu.VMEM((WIDTH, 2 * ROWS), BF), full(BF), one(F32),
        one(BF), one(BF), pltpu.VMEM((2, 2 * ROWS, HEAD), BF), blocks(4, F32),
        blocks(2, F32), one(jnp.int32),
        tall(ROWS, BF), pltpu.VMEM((ROWS, 2 * ROWS), F32), tall(ROWS, F32), full(BF),
        stats, blocks(NY, BF), one(F32), one(F32), one(F32), one(BF),
        pltpu.VMEM((ROWS, 2 * ROWS), BF), tall(HEAD, F32), tall(HEAD, F32),
        blocks(2, BF), blocks(2, BF),
        blocks(NY, F32), blocks(NY, BF), blocks(NY - 1, BF), stats,
        full(BF), one(BF), one(BF), tall(2 * HEAD, BF), pltpu.VMEM((2, WIDTH, ROWS), BF), blocks(2, BF),
        *reduce_scratch(NX, NZ, 16, BF),
        *reduce3_scratch(2 * HEAD),
        *reduce3_scratch(HEAD),
        pltpu.SemaphoreType.DMA((5,)),
        pltpu.SemaphoreType.DMA((5,)),
        pltpu.SemaphoreType.DMA((39,)),
        pltpu.SemaphoreType.DMA((39,)),
    ]
    rounded = (
        (ROWS, HEAD),
        (ROWS, HEAD),
        (NC, NZ, ROWS // (NC * NZ), 2 * HEAD),
        (NC, NZ, ROWS // (NC * NZ), HEAD),
        (NC, NX, NZ, 16, HEAD),
    )
    shapes = (
        jax.ShapeDtypeStruct((ROWS, HEAD), BF),
        jax.ShapeDtypeStruct((ROWS, HEAD), BF),
        jax.ShapeDtypeStruct((WIDTH, 4 * HEAD), F32),
        jax.ShapeDtypeStruct((HEAD, WIDTH), F32),
    )
    results = pl.pallas_call(
        kernel,
        out_shape=tuple(jax.ShapeDtypeStruct(shape, BF) for shape in rounded),
        in_specs=[hbm] * 5,
        out_specs=(hbm,) * 5,
        scratch_shapes=scratch,
        compiler_params=pltpu.CompilerParams(
            collective_id=0, has_side_effects=True, vmem_limit_bytes=62 * 1024 * 1024
        ),
        name="layer",
    )(tokens, lengths, weight_in, weight_out, grad_out)
    return pl.pallas_call(
        store,
        out_shape=shapes,
        in_specs=[hbm] * 5,
        out_specs=(hbm,) * 4,
        scratch_shapes=[pltpu.VMEM(shape, BF) for shape in rounded]
        + [full(F32), pltpu.VMEM((HEAD, WIDTH), F32)]
        + [pltpu.SemaphoreType.DMA((5,)), pltpu.SemaphoreType.DMA((7,))],
        compiler_params=pltpu.CompilerParams(vmem_limit_bytes=62 * 1024 * 1024),
        name="store",
    )(*results)


def solution(mesh):
    placed = (P("dp", "sub"), P(), P(None, "sub"), P("sub", None), P("dp", "sub"))
    return jax.shard_map(
        shards,
        mesh=mesh,
        in_specs=placed,
        out_specs=(P("dp", "sub"), P("dp", "sub"), P(None, "sub"), P("sub", None)),
        check_vma=False,
    )
```

```python
import functools
import math

import jax
import jax.numpy as jnp
from jax import lax
from jax.experimental import pallas as pl
from jax.experimental.pallas import tpu as pltpu
from jax.sharding import PartitionSpec as P

EPSILON = 1e-05
NX, NZ, NC, NY = 4, 8, 2, 4
ROWS, HEAD, WIDTH = 512, 128, 512
TILE = 128
MESH = pl.DeviceIdType.MESH
BF, F32 = jnp.bfloat16, jnp.float32

NN = (((1,), (0,)), ((), ()))
NT = (((1,), (1,)), ((), ()))
TN = (((0,), (0,)), ((), ()))


def mm(left, right, dims=NN):
    return lax.dot_general(left, right, dims, preferred_element_type=F32)


class Exchange:
    def __init__(self, make, whole):
        self.make, self.whole = make, whole

    def add(self, src, dst, device):
        self.make(src, dst, device).start()
        self.device = device
        return self

    def wait_recv(self):
        self.make(self.whole, self.whole, self.device).wait_recv()

    def wait_send(self):
        self.make(self.whole, self.whole, self.device).wait_send()


class Sender:
    def __init__(self, send_sem, recv_sem):
        self.send_sem, self.recv_sem, self.groups = send_sem, recv_sem, []

    def group(self, whole, copies=()):
        i = len(self.groups)

        def make(src, dst, device):
            return pltpu.make_async_remote_copy(
                src_ref=src,
                dst_ref=dst,
                send_sem=self.send_sem.at[i],
                recv_sem=self.recv_sem.at[i],
                device_id=device,
                device_id_type=MESH,
            )

        group = Exchange(make, whole)
        self.groups.append(group)
        for src, dst, device in copies:
            group.add(src, dst, device)
        return group

    def __call__(self, src, dst, device):
        return self.group(src, [(src, dst, device)])


def far_first(n):
    return sorted(range(1, n), key=lambda r: (-min(r, n - r), r))


class Reduce:
    def __init__(self, send, core, first, second, refs, scale):
        self.send, self.scale = send, scale
        self.c, self.core = core
        self.n1, self.i1, self.at1 = first
        self.n2, self.i2, self.at2 = second
        self.part, self.sb, self.rc, self.s_1, self.r_1, self.s_2, self.r_2, self.full = refs
        self.dt = self.full.dtype

    def to1(self, r):
        return lax.rem(self.i1 + r, self.n1)

    def to2(self, r):
        return lax.rem(self.i2 + r, self.n2)

    def s1(self, other):
        self.sb[...] = other.astype(self.dt).reshape(self.sb.shape)
        self.w1 = self.send(self.sb, self.rc, self.core)

    def keep(self, own):
        self.part[...] = own.reshape(self.part.shape)

    def s2(self):
        self.w1.wait_recv()
        total = self.part[...] + self.rc[...].astype(F32)
        self.part[...] = total
        self.s_1[...] = total.astype(self.dt)
        self.w2 = self.send.group(self.r_1)
        for r in far_first(self.n1):
            to = self.to1(r)
            self.w2.add(self.s_1.at[to], self.r_1.at[r - 1], self.at1(to))

    def s3(self):
        self.w2.wait_recv()
        total = self.part[self.i1]
        for r in range(self.n1 - 1):
            total = total + self.r_1[r].astype(F32)
        self.part[0] = total
        self.s_2[...] = total.astype(self.dt)
        self.w3 = self.send.group(self.r_2)
        for r in far_first(self.n2):
            to = self.to2(r)
            self.w3.add(self.s_2.at[to], self.r_2.at[r - 1], self.at2(to))

    def s4(self):
        self.w3.wait_recv()
        total = self.part[0, self.i2]
        for r in range(self.n2 - 1):
            total = total + self.r_2[r].astype(F32)
        mine = self.full.at[self.c, self.i1, self.i2]
        self.full[self.c, self.i1, self.i2] = (total * self.scale).astype(self.dt)
        self.w4 = self.send.group(
            self.r_2, [(mine, mine, self.at2(self.to2(r))) for r in far_first(self.n2)]
        )

    def s5(self):
        self.w4.wait_recv()
        mine = self.full.at[self.c, self.i1]
        self.w5 = [
            (r, self.send(mine, mine, self.at1(self.to1(r)))) for r in far_first(self.n1)
        ]
        self.w6 = self.send.group(self.s_1, [(mine, mine, self.core)])

    def s6(self):
        for r, w in self.w5[::-1]:
            w.wait_recv()
            piece = self.full.at[self.c, lax.rem(self.i1 + self.n1 - r, self.n1)]
            self.w6.add(piece, piece, self.core)

    def s7(self):
        self.w6.wait_recv()


class Reduce3:
    def __init__(self, send, core, first, second, refs, scale):
        self.send, self.scale = send, scale
        self.c, self.core = core
        self.n1, self.i1, self.at1 = first
        self.n2, self.i2, self.at2 = second
        self.part, self.sb, self.rc, self.s_1, self.r_1, self.both, self.full = refs
        self.dt = self.full.dtype

    def s1(self, other):
        self.sb[...] = other.astype(self.dt).reshape(self.sb.shape)
        self.w1 = self.send(self.sb, self.rc, self.core)

    def keep(self, own):
        self.part[...] = own.reshape(self.part.shape)

    def s2(self):
        self.w1.wait_recv()
        total = self.part[...] + self.rc[...].astype(F32)
        self.part[...] = total
        self.s_1[...] = total.astype(self.dt)
        self.w2 = self.send.group(self.r_1)
        for r in far_first(self.n1):
            to = lax.rem(self.i1 + r, self.n1)
            self.w2.add(self.s_1.at[to], self.r_1.at[r - 1], self.at1(to))

    def s3(self):
        self.w2.wait_recv()
        total = self.part[self.i1]
        for r in range(self.n1 - 1):
            total = total + self.r_1[r].astype(F32)
        self.both[self.i2] = total.astype(self.dt)
        mine = self.both.at[self.i2]
        self.w3 = self.send.group(
            self.both.at[0 : self.n2 - 1],
            [
                (mine, mine, self.at2(lax.rem(self.i2 + r, self.n2)))
                for r in far_first(self.n2)
            ],
        )

    def s4(self):
        self.w3.wait_recv()
        total = self.both[0].astype(F32)
        for k in range(1, self.n2):
            total = total + self.both[k].astype(F32)
        self.full[self.c, self.i1] = (total * self.scale).astype(self.dt)
        mine = self.full.at[self.c, self.i1]
        order = far_first(self.n1)
        self.w4 = []
        for steps in (order[:3], order[3:]):
            peers = [self.at1(lax.rem(self.i1 + r, self.n1)) for r in steps]
            whole = self.r_1.at[0 : len(steps)]
            self.w4.append((steps, self.send.group(whole, [(mine, mine, to) for to in peers])))
        self.w5 = self.send.group(self.s_1, [(mine, mine, self.core)])

    def s5(self):
        for steps, w in self.w4[::-1]:
            w.wait_recv()
            for r in steps:
                piece = self.full.at[self.c, lax.rem(self.i1 + self.n1 - r, self.n1)]
                self.w5.add(piece, piece, self.core)

    def s6(self):
        self.w5.wait_recv()


def column(value):
    return jnp.sum(value, axis=1, keepdims=True)


def start_rows(lens_ref, first_row):
    lens = jnp.broadcast_to(lens_ref[...].astype(F32), (128, 128))
    down = lax.broadcasted_iota(jnp.int32, (128, 128), 0)
    across = lax.broadcasted_iota(jnp.int32, (128, 128), 1)
    as_column = column(jnp.where(down == across, lens, 0.0))
    starts = jnp.sum(jnp.where(down < across, as_column, 0.0), axis=0, keepdims=True)
    rows = (first_row + lax.broadcasted_iota(jnp.int32, (ROWS, 128), 0)).astype(F32)
    own = jnp.max(jnp.where(starts <= rows, starts, 0.0), axis=1, keepdims=True)
    return own - first_row.astype(F32)


def kernel(
    tok_h, len_h, win_h, wout_h, gout_h,
    lo, gt, g_vk, g_q, g_uo,
    lens, win, wout, lo_v, gt_v,
    xg, gg, wc, xh, xn, xnt, xnp, xr, gate, qb, kv, slope, slope_p, srow,
    wt, sl, slt, wp,
    stat, gat, att, ee, dgate, datt, ds, dk, dv, dkv_s, dkv_r,
    din, din_s, din_r, stat2, dhid, dh_u, dh_q, dh_vk, left, right,
    *rest,
):
    reduce_refs, (load_sem, out_sem, send_sem, recv_sem) = rest[:-4], rest[-4:]
    d, y = lax.axis_index("dp"), lax.axis_index("sub")
    c = lax.rem(d, NC)
    z = lax.rem(d // NC, NZ)
    x = d // (NC * NZ)
    ndp = NX * NZ * NC

    def at(ax, az, ac):
        return ((ax * NZ + az) * NC + ac, y)

    above = (lax.rem(d + 1, ndp), y)
    below = (lax.rem(d + ndp - 1, ndp), y)
    y_peers = [(r, lax.rem(y + r, NY)) for r in (2, 1, 3)]
    y_up, y_down = lax.rem(y + 1, NY), lax.rem(y + NY - 1, NY)

    loads = [
        pltpu.make_async_copy(src, dst, load_sem.at[i])
        for i, (src, dst) in enumerate(
            [
                (tok_h, xg.at[y]), (gout_h, gg.at[y]), (len_h, lens),
                (win_h, win), (wout_h, wout),
            ]
        )
    ]
    for load in loads:
        load.start()
    stores = []

    def put(src, dst):
        copy = pltpu.make_async_copy(src, dst, out_sem.at[len(stores)])
        copy.start()
        stores.append(copy)

    barrier = pltpu.get_barrier_semaphore()
    greet = [at(x, lax.rem(z + r, NZ), c) for r in far_first(NZ)]
    greet += [at(lax.rem(x + r, NX), z, c) for r in far_first(NX)]
    greet += [(d, peer) for _, peer in y_peers]
    greet += [(lax.rem(d + ndp + 2 * c - 1, ndp), y)]
    greet += [at(x, z, 1 - c)]
    for device in greet:
        pl.semaphore_signal(barrier, inc=1, device_id=device, device_id_type=MESH)
    for load in loads:
        load.wait()
    pl.semaphore_wait(barrier, len(greet))

    send = Sender(send_sem, recv_sem)
    core = (c, at(x, z, 1 - c))
    along_x = (NX, x, lambda to: at(to, z, c))
    along_z = (NZ, z, lambda to: at(x, to, c))
    scaling = 1.0 / math.sqrt(ROWS * ndp)
    r_uo = Reduce(send, core, along_x, along_z, reduce_refs[0:8], scaling)
    r_vk = Reduce3(send, core, along_z, along_x, reduce_refs[8:15], scaling)
    r_q = Reduce3(send, core, along_z, along_x, reduce_refs[15:22], scaling)
    tiles = [slice(t * TILE, (t + 1) * TILE) for t in range(ROWS // TILE)]
    half = ROWS // 2
    low, high = slice(0, half), slice(half, ROWS)

    def gather(own, whole):
        return send.group(whole, [(own, own, (d, peer)) for _, peer in y_peers])

    got_x = [gather(xg.at[y, rows], xg.at[0 : NY - 1, rows]) for rows in tiles[:-1]]
    pass_up = send(gg.at[y, low], gg.at[y, low], (d, y_up))
    pass_down = send(gg.at[y, high], gg.at[y, high], (d, y_down))
    rows = tiles[-1]
    got_x.append(gather(xg.at[y, rows], xg.at[0 : NY - 1, rows]))
    got_g = send.group(
        gg.at[0:2],
        [
            (gg.at[y, high], gg.at[y, high], (d, y_up)),
            (gg.at[y, low], gg.at[y, low], (d, y_down)),
        ],
    )
    srow[...] = jnp.broadcast_to(
        start_rows(lens, d * ROWS).astype(jnp.int32), (ROWS, 128)
    )
    wc[y] = wout[:, pl.ds(pl.multiple_of(y * HEAD, HEAD), HEAD)]
    root = 1.0 / math.sqrt(HEAD)

    def attend(scores, begin, first, causal):
        scores = scores * root
        col = lax.broadcasted_iota(jnp.int32, scores.shape, 1) + first
        allowed = col >= begin
        if causal is not None:
            row = lax.broadcasted_iota(jnp.int32, scores.shape, 0) + causal
            allowed = allowed & (col <= row)
        sig = 0.5 * jnp.tanh(0.5 * scores) + 0.5
        weight = jnp.where(allowed, scores * sig, 0.0).astype(BF)
        tangent = jnp.where(allowed, sig * (1.0 + scores * (1.0 - sig)) * root, 0.0)
        return weight, tangent

    got_kv = []
    for t, rows in enumerate(tiles):
        if t == len(tiles) - 1:
            pass_up.wait_recv()
            slot = gg.at[y_down, low]
            got_g.add(slot, slot, (d, y_up))
            pass_down.wait_recv()
            slot = gg.at[y_up, high]
            got_g.add(slot, slot, (d, y_down))
        got_x[t].wait_recv()
        parts = [xg[b, rows].astype(F32) for b in range(NY)]
        mean = column(parts[0] + parts[1] + parts[2] + parts[3]) * (1.0 / WIDTH)
        parts = [part - mean for part in parts]
        var = column(sum(part * part for part in parts)) * (1.0 / WIDTH)
        inv = lax.rsqrt(var + EPSILON)
        xr[rows, :] = jnp.broadcast_to(inv, (TILE, 128))
        for b in range(NY):
            hat = parts[b] * inv
            xh[b, rows] = hat
            xn[rows, b * HEAD : (b + 1) * HEAD] = hat.astype(BF)
        hidden = mm(xn[rows, :], win[...])
        sig = 0.5 * jnp.tanh(0.5 * hidden) + 0.5
        projected = (hidden * sig).astype(BF)
        own = slice(ROWS + t * TILE, ROWS + (t + 1) * TILE)
        kv[0, own] = projected[:, HEAD : 2 * HEAD]
        kv[1, own] = projected[:, 3 * HEAD :]
        got_kv.append(send(kv.at[:, own], kv.at[:, rows], above))
        gate[rows, :] = projected[:, :HEAD]
        qb[rows, :] = projected[:, 2 * HEAD : 3 * HEAD]
        slopes = sig * (1.0 + hidden * (1.0 - sig))
        for i, g in enumerate((0, 2, 1, 3)):
            slope[i, rows] = slopes[:, g * HEAD : (g + 1) * HEAD]

    for t, rows in enumerate(tiles):
        weight, tangent = attend(
            mm(qb[rows, :], kv[1, ROWS:], NT), srow[rows, 0:1], 0, t * TILE
        )
        wt[ROWS:, rows] = weight.T
        sl[rows, ROWS:] = tangent
        slt[ROWS:, rows] = tangent.T
        att[rows, :] = mm(weight, kv[0, ROWS:])
    got_xn = [send(xn.at[rows], xnp.at[rows], above) for rows in (low, high)]
    xnt[:, ROWS:] = xn[...].T

    for t, cols in enumerate(tiles):
        got_kv[t].wait_recv()
        weight, tangent = attend(
            mm(qb[...], kv[1, cols], NT), srow[...], t * TILE - ROWS, None
        )
        wp[:, cols] = weight
        sl[:, cols] = tangent
        att[...] = att[...] + mm(weight, kv[0, cols])

    got_g.wait_recv()
    d_gated = sum(
        mm(gg[b], wout[:, b * HEAD : (b + 1) * HEAD], NT) for b in range(NY)
    )
    dgate[...] = d_gated
    e = d_gated * gate[...].astype(F32)
    ee[...] = e

    a = att[...]
    sum_a = column(a)
    ca = a - sum_a * (1.0 / HEAD)
    lane = lax.broadcasted_iota(jnp.int32, (ROWS, 128), 1)
    packed = jnp.where(
        lane == 0, sum_a,
        jnp.where(lane == 1, column(ca * ca),
                  jnp.where(lane == 2, column(e), jnp.where(lane == 3, column(e * ca), 0.0))),
    )
    stat[y] = packed.T[:8]
    got_s = gather(stat.at[y], stat.at[0 : NY - 1])
    for rows in tiles:
        wt[rows, :] = wp[:, rows].T
        slt[rows, :] = sl[:, rows].T
    def block_before(t, rows):
        got_xn[t].wait_recv()
        for i, g in enumerate((1, 3)):
            hidden = mm(xnp[rows, :], win[:, g * HEAD : (g + 1) * HEAD])
            sig = 0.5 * jnp.tanh(0.5 * hidden) + 0.5
            slope_p[i, rows] = sig * (1.0 + hidden * (1.0 - sig))
        xnt[:, rows] = xnp[rows, :].T

    for b in range(NY):
        left[1, b * HEAD : (b + 1) * HEAD] = gg[b].T
    left[0] = xnt[:, ROWS:]
    block_before(0, low)
    got_s.wait_recv()
    heads = [stat[h] for h in range(NY)]
    mean = sum(h[0:1] for h in heads) * (1.0 / WIDTH)
    var, s_e, s_en = 0.0, 0.0, 0.0
    for h in heads:
        off = h[0:1] * (1.0 / HEAD) - mean
        var = var + h[1:2] + HEAD * off * off
        s_e = s_e + h[2:3]
        s_en = s_en + h[3:4] + off * h[2:3]
    inv = lax.rsqrt(var * (1.0 / WIDTH) + EPSILON)
    line = lax.broadcasted_iota(jnp.int32, (128, ROWS), 0)
    back = jnp.where(
        line == 0, mean,
        jnp.where(line == 1, inv,
                  jnp.where(line == 2, s_e * (1.0 / WIDTH),
                            jnp.where(line == 3, s_en * inv * (1.0 / WIDTH), 0.0))),
    ).T
    mean, inv, s_e, s_en = [back[:, i : i + 1] for i in range(4)]
    normed = (att[...] - mean) * inv
    datt[...] = (inv * (ee[...] - s_e - normed * s_en)).astype(BF)
    gat[y] = (normed * gate[...].astype(F32)).astype(BF)
    got_a = gather(gat.at[y], gat.at[0 : NY - 1])
    got_w = send.group(
        wc.at[0 : NY - 1],
        [
            (
                wout.at[:, pl.ds(pl.multiple_of(peer * HEAD, HEAD), HEAD)],
                wc.at[y],
                (d, peer),
            )
            for _, peer in y_peers
        ],
    )
    dh_u[...] = (dgate[...] * normed * slope[0]).astype(BF)

    right[0] = dh_u[...]
    right[1] = gat[y]
    r_uo.s1(mm(left[1 - c], right[1 - c]))

    def key_grads(rows, first):
        d_st = (mm(kv[0, rows], datt[first:, :], NT) * slt[rows, first:]).astype(BF)
        dk[rows, :] = mm(d_st, qb[first:, :])
        dv[rows, :] = mm(wt[rows, first:], datt[first:, :])

    for t in range(ROWS // TILE):
        key_grads(tiles[t], 0)
    dkv_s[0] = dv[:ROWS, :].astype(BF)
    dkv_s[1] = dk[:ROWS, :].astype(BF)
    got_dkv = send(dkv_s, dkv_r, below)
    r_uo.keep(mm(left[c], right[c]))
    r_uo.s2()
    for t in range(ROWS // TILE):
        key_grads(slice(ROWS + t * TILE, ROWS + (t + 1) * TILE), t * TILE)

    block_before(1, high)
    dh_vk[:ROWS, :HEAD] = (dv[:ROWS, :] * slope_p[0]).astype(BF)
    dh_vk[:ROWS, HEAD:] = (dk[:ROWS, :] * slope_p[1]).astype(BF)
    dh_vk[ROWS:, :HEAD] = (dv[ROWS:, :] * slope[2]).astype(BF)
    dh_vk[ROWS:, HEAD:] = (dk[ROWS:, :] * slope[3]).astype(BF)
    mine = pl.ds(pl.multiple_of(c * half, half), half)
    theirs = pl.ds(pl.multiple_of((1 - c) * half, half), half)
    r_vk.s1(mm(xnt[theirs, :], dh_vk[...]))

    for rows in tiles:
        ds[rows, :] = (mm(datt[rows, :], kv[0], NT) * sl[rows, :]).astype(BF)
        dq = mm(ds[rows, :], kv[1])
        dh_q[rows, :] = (dq * slope[1, rows]).astype(BF)
    r_q.s1(mm(xnt[theirs, ROWS:], dh_q[...]))
    r_vk.keep(mm(xnt[mine, :], dh_vk[...]))
    r_vk.s2()
    r_q.keep(mm(xnt[mine, ROWS:], dh_q[...]))
    r_q.s2()
    r_uo.s3()

    dhid[:, 0:HEAD] = dh_u[...]
    dhid[:, 2 * HEAD : 3 * HEAD] = dh_q[...]
    got_dkv.wait_recv()
    dhid[:, HEAD : 2 * HEAD] = ((dv[ROWS:, :] + dkv_r[0].astype(F32)) * slope[2]).astype(BF)
    dhid[:, 3 * HEAD :] = ((dk[ROWS:, :] + dkv_r[1].astype(F32)) * slope[3]).astype(BF)
    one, two = 0.0, 0.0
    for b in range(NY):
        part = mm(dhid[...], win[b * HEAD : (b + 1) * HEAD, :], NT)
        one = one + part
        two = two + part * xh[b]
        din[b] = part
        din_s[b] = part.astype(BF)
    packed = jnp.where(lane == 0, column(one), jnp.where(lane == 1, column(two), 0.0))
    stat2[y] = packed.T[:8]
    got_i = send.group(
        din_r, [(din_s.at[peer], din_r.at[r - 1], (d, peer)) for r, peer in y_peers]
    )
    got_t = gather(stat2.at[y], stat2.at[0 : NY - 1])

    got_a.wait_recv()
    got_w.wait_recv()
    lo_v[...] = (
        xg[y].astype(F32) + sum(mm(gat[h], wc[h]) for h in range(NY))
    ).astype(BF)
    put(lo_v, lo)
    r_vk.s3()
    r_uo.s4()
    r_q.s3()
    r_vk.s4()
    r_q.s4()
    r_uo.s5()

    got_i.wait_recv()
    got_t.wait_recv()
    total = din[y]
    for r in range(NY - 1):
        total = total + din_r[r].astype(F32)
    both = (stat2[0] + stat2[1] + stat2[2] + stat2[3]) * (1.0 / WIDTH)
    back = jnp.where(line == 0, both[0:1], jnp.where(line == 1, both[1:2], 0.0)).T
    piece = xr[:, 0:1] * (total - back[:, 0:1] - xh[y] * back[:, 1:2])
    gt_v[...] = (gg[y].astype(F32) + piece).astype(BF)
    put(gt_v, gt)

    r_vk.s5()
    r_q.s5()
    r_uo.s6()
    r_vk.s6()
    put(r_vk.full, g_vk)
    r_q.s6()
    put(r_q.full, g_q)
    r_uo.s7()
    put(r_uo.full, g_uo)
    for w in send.groups:
        w.wait_send()
    for w in stores:
        w.wait()


def store(
    lo_h, gt_h, vk_h, q_h, uo_h, lo, gt, gwin, gwout,
    lo_v, gt_v, vk, q, uo, gwin_v, gwout_v, read_sem, write_sem,
):
    pairs = [(lo_h, lo_v), (gt_h, gt_v), (vk_h, vk), (q_h, q), (uo_h, uo)]
    reads = [
        pltpu.make_async_copy(src, dst, read_sem.at[i]) for i, (src, dst) in enumerate(pairs)
    ]
    writes = []

    def write(src, dst):
        writes.append(pltpu.make_async_copy(src, dst, write_sem.at[len(writes)]))
        writes[-1].start()

    def write_columns(g, value):
        cols = slice(g * HEAD, (g + 1) * HEAD)
        gwin_v[:, cols] = value.reshape(ROWS, HEAD).astype(F32)
        write(gwin_v.at[:, cols], gwin.at[:, cols])

    for i in (4, 2, 3, 0, 1):
        reads[i].start()
    reads[4].wait()
    write_columns(0, uo[0])
    gwout_v[...] = uo[1].reshape(WIDTH, HEAD).astype(F32).T
    write(gwout_v, gwout)
    reads[2].wait()
    write_columns(1, vk[:, :, :, :HEAD])
    write_columns(3, vk[:, :, :, HEAD:])
    reads[3].wait()
    write_columns(2, q[...])
    reads[0].wait()
    write(lo_v, lo)
    reads[1].wait()
    write(gt_v, gt)
    for copy in writes:
        copy.wait()


def reduce3_scratch(n):
    r = ROWS // (NC * NZ)
    block = (NZ, r, n)
    return [
        pltpu.VMEM(block, F32),
        pltpu.VMEM(block, BF),
        pltpu.VMEM(block, BF),
        pltpu.VMEM(block, BF),
        pltpu.VMEM((NZ - 1, r, n), BF),
        pltpu.VMEM((NX, r, n), BF),
        pltpu.VMEM((NC,) + block, BF),
    ]


def reduce_scratch(n1, n2, rows, dt):
    block = (n1, n2, rows, HEAD)
    return [
        pltpu.VMEM(block, F32),
        pltpu.VMEM(block, dt),
        pltpu.VMEM(block, dt),
        pltpu.VMEM(block, dt),
        pltpu.VMEM((n1 - 1, n2, rows, HEAD), dt),
        pltpu.VMEM((n2, rows, HEAD), dt),
        pltpu.VMEM((n2 - 1, rows, HEAD), dt),
        pltpu.VMEM((NC,) + block, dt),
    ]


def shards(tokens, lengths, weight_in, weight_out, grad_out):
    lengths = lengths.reshape(1, -1)
    hbm = pl.BlockSpec(memory_space=pltpu.HBM)
    blocks = lambda n, dt: pltpu.VMEM((n, ROWS, HEAD), dt)
    full = lambda dt: pltpu.VMEM((ROWS, WIDTH), dt)
    one = lambda dt: pltpu.VMEM((ROWS, HEAD), dt)
    tall = lambda n, dt: pltpu.VMEM((2 * ROWS, n), dt)
    stats = pltpu.VMEM((NY, 8, ROWS), F32)
    scratch = [
        pltpu.VMEM((1, 128), jnp.int32), full(BF), pltpu.VMEM((HEAD, WIDTH), BF),
        one(BF), one(BF),
        blocks(NY, BF), blocks(NY, BF), pltpu.VMEM((NY, HEAD, HEAD), BF),
        blocks(NY, F32), full(BF), pltpu.VMEM((WIDTH, 2 * ROWS), BF), full(BF), one(F32),
        one(BF), one(BF), pltpu.VMEM((2, 2 * ROWS, HEAD), BF), blocks(4, F32),
        blocks(2, F32), one(jnp.int32),
        tall(ROWS, BF), pltpu.VMEM((ROWS, 2 * ROWS), F32), tall(ROWS, F32), full(BF),
        stats, blocks(NY, BF), one(F32), one(F32), one(F32), one(BF),
        pltpu.VMEM((ROWS, 2 * ROWS), BF), tall(HEAD, F32), tall(HEAD, F32),
        blocks(2, BF), blocks(2, BF),
        blocks(NY, F32), blocks(NY, BF), blocks(NY - 1, BF), stats,
        full(BF), one(BF), one(BF), tall(2 * HEAD, BF), pltpu.VMEM((2, WIDTH, ROWS), BF), blocks(2, BF),
        *reduce_scratch(NX, NZ, 16, BF),
        *reduce3_scratch(2 * HEAD),
        *reduce3_scratch(HEAD),
        pltpu.SemaphoreType.DMA((5,)),
        pltpu.SemaphoreType.DMA((5,)),
        pltpu.SemaphoreType.DMA((39,)),
        pltpu.SemaphoreType.DMA((39,)),
    ]
    rounded = (
        (ROWS, HEAD),
        (ROWS, HEAD),
        (NC, NZ, ROWS // (NC * NZ), 2 * HEAD),
        (NC, NZ, ROWS // (NC * NZ), HEAD),
        (NC, NX, NZ, 16, HEAD),
    )
    shapes = (
        jax.ShapeDtypeStruct((ROWS, HEAD), BF),
        jax.ShapeDtypeStruct((ROWS, HEAD), BF),
        jax.ShapeDtypeStruct((WIDTH, 4 * HEAD), F32),
        jax.ShapeDtypeStruct((HEAD, WIDTH), F32),
    )
    results = pl.pallas_call(
        kernel,
        out_shape=tuple(jax.ShapeDtypeStruct(shape, BF) for shape in rounded),
        in_specs=[hbm] * 5,
        out_specs=(hbm,) * 5,
        scratch_shapes=scratch,
        compiler_params=pltpu.CompilerParams(
            collective_id=0, has_side_effects=True, vmem_limit_bytes=62 * 1024 * 1024
        ),
        name="layer",
    )(tokens, lengths, weight_in, weight_out, grad_out)
    return pl.pallas_call(
        store,
        out_shape=shapes,
        in_specs=[hbm] * 5,
        out_specs=(hbm,) * 4,
        scratch_shapes=[pltpu.VMEM(shape, BF) for shape in rounded]
        + [full(F32), pltpu.VMEM((HEAD, WIDTH), F32)]
        + [pltpu.SemaphoreType.DMA((5,)), pltpu.SemaphoreType.DMA((7,))],
        compiler_params=pltpu.CompilerParams(vmem_limit_bytes=62 * 1024 * 1024),
        name="store",
    )(*results)


def solution(mesh):
    placed = (P("dp", "sub"), P(), P(None, "sub"), P("sub", None), P("dp", "sub"))
    return jax.shard_map(
        shards,
        mesh=mesh,
        in_specs=placed,
        out_specs=(P("dp", "sub"), P("dp", "sub"), P(None, "sub"), P("sub", None)),
        check_vma=False,
    )
```
